128 devices in a mesh: ctx: 32 (over x, y, core), head: 4 (over z).
Axes of the slice: x: 4, y: 4, z: 4, core: 2. Of those that a mesh axis runs over, the one named last changes fastest.
Arguments:
- queries: bfloat16 [16384, 1024], P('ctx', 'head')
- keys: bfloat16 [16384, 128], P('ctx')
- values: bfloat16 [16384, 128], P('ctx'), may hold values from -6 to 6
- doc_ids: int32 [16384], P('ctx'), may hold values from 0 to 3, never falling along the last dimension, each value on 1 to 12288 neighbouring positions
- out_grad: bfloat16 [16384, 1024], P('ctx', 'head'), may hold values from -6 to 6
Outputs:
- attn_out: bfloat16 [16384, 1024], P('ctx', 'head')
- q_grad: float32 [16384, 1024], P('ctx', 'head')
- k_grad: float32 [16384, 128], P('ctx')
- v_grad: float32 [16384, 128], P('ctx')
The draws below stay inside these ranges and needn't reach their ends.
Inputs may be any that keep to these rules, and one draw needn't show every extreme that they name: doc_ids never fall along the tokens; every document has 1 to 12288 tokens and one has exactly 12288.
All inputs are finite; a program needn't handle non-finite values.
Results may differ from the reference program's by a relative error of at most 0.018.
Values may be sent and summed in bfloat16 or wider, within the bound.
No kernel may reach another device: no remote copies, remote signals or barrier semaphores. Data moves between devices by JAX's collectives and lax.ppermute only.
A program may use at most 128 MiB of HBM per device.

```python
import math
import jax
import jax.numpy as jnp
import numpy as np
from jax import lax

HEADS = 8
DH = 128
DOCS = 4
TOKENS = 16384
MAXDOC = 12288


def shared_keys(key):
    return jax.random.normal(jax.random.fold_in(key, 11), (TOKENS, DH), jnp.float32)


def draw_keys(key, part):
    base = shared_keys(key)
    return base.astype(jnp.bfloat16)


def draw_queries(key, part):
    key = jax.random.fold_in(key, 5)
    fresh = jax.random.normal(key, (TOKENS, HEADS, DH), jnp.float32)
    return fresh.reshape(TOKENS, HEADS * DH).astype(jnp.bfloat16)


def levels(stream_key, dims, shards, least, largest):
    gain = 1.0
    for position, parts in shards:
        steps = jax.random.uniform(jax.random.fold_in(jax.random.fold_in(stream_key, 6), position), (parts,), jnp.float32, least / len(shards), largest / len(shards))
        gain = gain * jnp.repeat(jnp.exp(steps), dims[position] // parts).reshape((-1,) + (1,) * (len(dims) - 1 - position))
    return gain


def profile(number_of, total, most, lean):
    weights = [(1 << 20) // math.isqrt(rank ** lean) + 1 for rank in range(2, number_of + 1)]
    surplus, given = total - most - (number_of - 1), [1] * (number_of - 1)
    while surplus > 0:
        candidates = [i for i in range(number_of - 1) if given[i] < most]
        mass, left = sum([weights[i] for i in candidates]), surplus
        for i in candidates:
            more = min(most - given[i], max(1, left * weights[i] // mass), surplus)
            given[i] = given[i] + more
            surplus = surplus - more
    return np.array([most] + given)


def uneven(own_key, count, total, bound, skew):
    if count == 2:
        one = jax.random.randint(own_key, (), max(1, total - bound), min(bound, total - 1) + 1)
        return jnp.stack([one, total - one])
    lengths = jnp.asarray(profile(count, total, bound, skew), jnp.int32)
    couples = (count - 1) // 2
    source_of, sink = lengths[1:1 + 2 * couples:2], lengths[2:2 + 2 * couples:2]
    slack = jnp.minimum(source_of - 1, bound - sink)
    shifted = jax.random.randint(jax.random.fold_in(own_key, 1), (couples,), 0, 1 << 20) % (slack + 1)
    lengths = lengths.at[1:1 + 2 * couples:2].set(source_of - shifted).at[2:2 + 2 * couples:2].set(sink + shifted)
    return lengths[jax.random.permutation(jax.random.fold_in(own_key, 2), count)]


def centred(key, shape, scale, reach, shards=(), kind=jnp.bfloat16):
    values = jax.random.normal(key, shape, jnp.float32) * scale
    if len(shards) > 0:
        values = levels(key, shape, shards, -0.22, 0.18) * values
    return jnp.clip(values, min=-reach, max=reach).astype(kind)


def setup_inputs(seed: int = 0) -> dict:
    streams_of = jax.random.split(jax.random.key(seed), 6)
    return {
        "queries": draw_queries(jax.random.fold_in(streams_of[5], 71), 0),
        "keys": draw_keys(jax.random.fold_in(streams_of[5], 71), 0),
        "values": centred(streams_of[2], (TOKENS, DH), 1.0, 6.0, ((0, 32),)),
        "doc_ids": jnp.searchsorted(jnp.cumsum(uneven(streams_of[3], DOCS, TOKENS, MAXDOC, 2)), jnp.arange(TOKENS), side="right").astype(jnp.int32),
        "out_grad": centred(streams_of[4], (TOKENS, HEADS * DH), 1.0, 6.0, ((0, 32), (1, 4))),
    }


def rounded(array):
    return lax.optimization_barrier(array.astype(jnp.bfloat16)).astype(jnp.float32)


def reference(queries, keys, values, doc_ids, out_grad):
    scale = DH ** -0.5
    block = math.gcd(TOKENS, 512)
    nblock = TOKENS // block
    hi = lax.Precision.HIGHEST
    pos = jnp.arange(TOKENS, dtype=jnp.int32)
    qall = queries.astype(jnp.float32).reshape(TOKENS, HEADS, DH)
    gall = out_grad.astype(jnp.float32).reshape(TOKENS, HEADS, DH)
    kall = keys.astype(jnp.float32)
    vall = values.astype(jnp.float32)

    def allowed(qpos, qdoc, kpos, kdoc):
        return (qdoc[:, None] == kdoc[None, :]) & (kpos[None, :] <= qpos[:, None])

    def forward(args):
        qblock, qpos, qdoc = args
        score = jnp.einsum('qhd,kd->hqk', qblock, kall, precision=hi) * scale
        keep = allowed(qpos, qdoc, pos, doc_ids)[None]
        score = jnp.where(keep, score, -1e30)
        rowmax = jnp.max(score, axis=-1)
        weights = jnp.where(keep, jnp.exp(score - rowmax[..., None]), 0.0)
        total = jnp.sum(weights, axis=-1)
        outb = jnp.einsum('hqk,kd->qhd', rounded(weights), vall, precision=hi) / total.T[..., None]
        return outb, rowmax + jnp.log(total)

    outs, lse = lax.map(forward, (qall.reshape(nblock, block, HEADS, DH), pos.reshape(nblock, block), doc_ids.reshape(nblock, block)))
    attn_out = outs.reshape(TOKENS, HEADS * DH).astype(jnp.bfloat16)
    lse_all = jnp.transpose(lse, (1, 0, 2)).reshape(HEADS, TOKENS)
    delta_all = jnp.sum(gall * attn_out.astype(jnp.float32).reshape(TOKENS, HEADS, DH), axis=-1).T

    def grads_of(qb, gb, qpos, qdoc, lseb, deltab, kb, vb, kpos, kdoc):
        score = jnp.einsum('qhd,kd->hqk', qb, kb, precision=hi) * scale
        keep = allowed(qpos, qdoc, kpos, kdoc)[None]
        probs = jnp.where(keep, jnp.exp(score - lseb[..., None]), 0.0)
        dprobs = jnp.einsum('qhd,kd->hqk', gb, vb, precision=hi)
        return probs, probs * (dprobs - deltab[..., None])

    def query_side(args):
        qb, gb, qpos, qdoc, lseb, deltab = args
        probs, dscore = grads_of(qb, gb, qpos, qdoc, lseb, deltab, kall, vall, pos, doc_ids)
        return jnp.einsum('hqk,kd->qhd', rounded(dscore), kall, precision=hi) * scale

    q_grad = lax.map(query_side, (qall.reshape(nblock, block, HEADS, DH), gall.reshape(nblock, block, HEADS, DH), pos.reshape(nblock, block), doc_ids.reshape(nblock, block), jnp.transpose(lse_all.reshape(HEADS, nblock, block), (1, 0, 2)), jnp.transpose(delta_all.reshape(HEADS, nblock, block), (1, 0, 2))))

    def key_side(args):
        kb, vb, kpos, kdoc = args
        probs, dscore = grads_of(qall, gall, pos, doc_ids, lse_all, delta_all, kb, vb, kpos, kdoc)
        kg = jnp.einsum('hqk,qhd->kd', rounded(dscore), qall, precision=hi) * scale
        vg = jnp.einsum('hqk,qhd->kd', rounded(probs), gall, precision=hi)
        return kg, vg

    k_grad, v_grad = lax.map(key_side, (kall.reshape(nblock, block, DH), vall.reshape(nblock, block, DH), pos.reshape(nblock, block), doc_ids.reshape(nblock, block)))
    return attn_out, q_grad.reshape(TOKENS, HEADS * DH), k_grad.reshape(TOKENS, DH), v_grad.reshape(TOKENS, DH)
```

```python
import functools
import math

import jax
import jax.numpy as jnp
from jax import lax
from jax.experimental import pallas as pl
from jax.experimental.pallas import tpu as pltpu
from jax.sharding import Mesh, PartitionSpec as P

BF = jnp.bfloat16
F32 = jnp.float32
DH = 128
ROWS = 512
CH = 128
NB = 32
HH = 2
RG = 256
NG = ROWS // RG
L = HH * RG
TF = 4
TB = 2
PAD = 4
SLOT = (0, 1, 3, 2)
LOW = -1e30
COEF = DH**-0.5 * math.log2(math.e)
XY = ("x", "y")


def load_keys(own_ref, other_ref, core, k_s, v_s, kt_s, vt_s):
    for c in range(NB // 2):
        for ref, par in ((own_ref, core), (other_ref, 1 - core)):
            at = pl.multiple_of((2 * c + par) * CH, CH)
            kc = ref[c, :CH, :DH]
            vc = ref[c, :CH, DH:]
            k_s[pl.ds(at, CH), :] = kc
            if v_s is not None:
                v_s[pl.ds(at, CH), :] = vc
            if kt_s is not None:
                kt_s[:, pl.ds(at, CH)] = kc.T
            if vt_s is not None:
                vt_s[:, pl.ds(at, CH)] = vc.T
    tail = NB * CH
    k_s[tail:, :] = jnp.zeros((PAD * CH, DH), BF)
    if v_s is not None:
        v_s[tail:, :] = jnp.zeros((PAD * CH, DH), BF)
    if kt_s is not None:
        kt_s[:, tail:] = jnp.zeros((DH, PAD * CH), BF)
    if vt_s is not None:
        vt_s[:, tail:] = jnp.zeros((DH, PAD * CH), BF)


def doc_starts(own_ref, other_ref):
    docs = jnp.concatenate(
        [own_ref[:, CH : CH + 16, :], other_ref[:, CH : CH + 16, :]], axis=0
    ).astype(F32)
    return [jnp.sum(jnp.where(docs < d, 1.0, 0.0)).astype(jnp.int32) for d in (1, 2, 3)]


def start_of(pos, starts):
    begin = jnp.zeros_like(pos)
    for c in starts:
        begin = jnp.where(pos >= c, c, begin)
    return begin


def group_facts(meta, gi, starts, step):
    x, y, core = meta[0], meta[1], meta[2]
    slot = gi // NG
    r = gi % NG
    back = jnp.where(slot == 2, 3, jnp.where(slot == 3, 2, slot))
    xs = (x - back + 4) % 4
    row0 = (8 * xs + 2 * y + core) * ROWS + r * RG
    lane = lax.broadcasted_iota(jnp.int32, (1, L), 1)
    rpos = row0 + lane % RG
    ds = start_of(rpos, starts)
    ds_min = start_of(row0, starts)
    ds_max = start_of(row0 + RG - 1, starts)
    lo = (ds_min - CH * x + (ROWS - CH)) // ROWS
    end = (row0 + RG - 1 - CH * x + ROWS) // ROWS
    tiles = jnp.maximum(0, (end - lo + step - 1) // step)
    return slot, r, xs, row0, rpos, ds, ds_max, lo, tiles


def group_rows(ref, slot, first, r):
    at = pl.multiple_of(first + r * RG, RG)
    both = ref[slot, pl.ds(at, RG), :]
    return both[:, :DH], both[:, DH:]


def keep_of(m0, x, rpos, ds, step):
    base = m0 * ROWS + x * CH
    i = lax.broadcasted_iota(jnp.int32, (step * CH, 1), 0)
    kpos = base + i + (ROWS - CH) * (i // CH)
    return (kpos <= rpos) & (kpos >= ds)


def mm(a, b):
    return jnp.dot(a, b, preferred_element_type=F32)


def forward_kernel(
    meta, own_ref, other_ref, a0, a1, a2, a3, ot_ref, st_ref, qg_s, k_s, vt_s, acc_s, m_s, l_s
):
    x, core = meta[0], meta[2]
    for s, ref in enumerate((a0, a1, a2, a3)):
        qg_s[s] = ref[...]
    load_keys(own_ref, other_ref, core, k_s, None, None, vt_s)
    starts = doc_starts(own_ref, other_ref)

    def group(gi, carry):
        slot, r, xs, row0, rpos, ds, ds_max, lo, tiles = group_facts(meta, gi, starts, TF)
        q0, q1 = group_rows(qg_s, slot, 0, r)
        qt = jnp.concatenate([q0.T, q1.T], axis=1)
        acc_s[...] = jnp.zeros_like(acc_s)
        m_s[...] = jnp.full_like(m_s, LOW)
        l_s[...] = jnp.zeros_like(l_s)

        def tile(i, carry):
            m0 = lo + i * TF
            at = pl.multiple_of(m0 * CH, CH)

            def work(masked):
                kt = k_s[pl.ds(at, TF * CH), :]
                s = mm(kt, qt)
                if masked:
                    keep = keep_of(m0, x, rpos, ds, TF)
                    s = jnp.where(keep, s, LOW)
                m_old = m_s[...]
                m_new = jnp.maximum(m_old, jnp.max(s, axis=0, keepdims=True) * COEF)
                alpha = jnp.exp2(m_old - m_new)
                p = jnp.exp2(s * COEF - m_new)
                if masked:
                    p = jnp.where(keep, p, 0.0)
                l_s[...] = l_s[...] * alpha + jnp.sum(p, axis=0, keepdims=True)
                m_s[...] = m_new
                acc_s[...] = acc_s[...] * alpha + mm(vt_s[:, pl.ds(at, TF * CH)], p.astype(BF))

            whole = ((m0 + TF - 1) * ROWS + x * CH + CH - 1 <= row0) & (
                m0 * ROWS + x * CH >= ds_max
            )
            pl.when(whole)(functools.partial(work, False))
            pl.when(jnp.logical_not(whole))(functools.partial(work, True))
            return carry

        lax.fori_loop(0, tiles, tile, 0)
        g0, g1 = group_rows(qg_s, slot, ROWS, r)
        gt = jnp.concatenate([g0.T, g1.T], axis=1).astype(F32)
        acc = acc_s[...]
        l = l_s[...]
        lanes = pl.ds(pl.multiple_of(r * L, L), L)
        ot_ref[slot, :, lanes] = (acc / jnp.where(l > 0, l, 1.0)).astype(BF)
        st_ref[xs, 0:1, lanes] = m_s[...]
        st_ref[xs, 1:2, lanes] = l
        st_ref[xs, 2:3, lanes] = jnp.sum(acc * gt, axis=0, keepdims=True)
        return carry

    lax.fori_loop(0, 4 * NG, group, 0)


def merged(sts):
    top = functools.reduce(jnp.maximum, [st[0:1] for st in sts])
    scale = [jnp.exp2(st[0:1] - top) for st in sts]
    total = sum(st[1:2] * f for st, f in zip(sts, scale))
    delta = sum(st[2:3] * f for st, f in zip(sts, scale)) / total
    parts = [st[1:2] * f / total for st, f in zip(sts, scale)]
    return top + jnp.log2(total), delta, parts


def backward_kernel(
    meta, own_ref, other_ref, a0, a1, a2, a3, s0, s1, s2, s3,
    dq_ref, mine_ref, theirs_ref, qg_s, k_s, v_s, kt_s, dk_s, dv_s, acc_s,
):
    x, core = meta[0], meta[2]
    for s, ref in enumerate((a0, a1, a2, a3)):
        qg_s[s] = ref[...]
    load_keys(own_ref, other_ref, core, k_s, v_s, kt_s, None)
    starts = doc_starts(own_ref, other_ref)
    dk_s[...] = jnp.zeros_like(dk_s)
    dv_s[...] = jnp.zeros_like(dv_s)

    def group(gi, carry):
        slot, r, xs, row0, rpos, ds, ds_max, lo, tiles = group_facts(meta, gi, starts, TB)
        q0, q1 = group_rows(qg_s, slot, 0, r)
        g0, g1 = group_rows(qg_s, slot, ROWS, r)
        qt = jnp.concatenate([q0.T, q1.T], axis=1)
        gt = jnp.concatenate([g0.T, g1.T], axis=1)
        qm = jnp.concatenate([q0, q1], axis=0)
        gm = jnp.concatenate([g0, g1], axis=0)
        lanes = pl.ds(pl.multiple_of(r * L, L), L)
        lse, delta, _ = merged([st[xs, :, lanes] for st in (s0, s1, s2, s3)])
        acc_s[...] = jnp.zeros_like(acc_s)

        def tile(i, carry):
            m0 = lo + i * TB
            at = pl.multiple_of(m0 * CH, CH)
            here = pl.ds(at, TB * CH)

            def work(masked):
                s = mm(k_s[here, :], qt)
                p = jnp.exp2(s * COEF - lse)
                if masked:
                    p = jnp.where(keep_of(m0, x, rpos, ds, TB), p, 0.0)
                dp = mm(v_s[here, :], gt)
                dsc = (p * (dp - delta)).astype(BF)
                dv_s[here, :] += mm(p.astype(BF), gm)
                dk_s[here, :] += mm(dsc, qm)
                acc_s[...] += mm(kt_s[:, here], dsc)

            whole = ((m0 + TB - 1) * ROWS + x * CH + CH - 1 <= row0) & (
                m0 * ROWS + x * CH >= ds_max
            )
            pl.when(whole)(functools.partial(work, False))
            pl.when(jnp.logical_not(whole))(functools.partial(work, True))
            return carry

        lax.fori_loop(0, tiles, tile, 0)
        acc = acc_s[...]
        rows_at = pl.ds(pl.multiple_of(r * RG, RG), RG)
        for h in range(HH):
            part = acc[:, h * RG : (h + 1) * RG].T
            dq_ref[slot, rows_at, h * DH : (h + 1) * DH] = part.astype(BF)
        return carry

    lax.fori_loop(0, 4 * NG, group, 0)
    for c in range(NB // 2):
        for ref, par in ((mine_ref, core), (theirs_ref, 1 - core)):
            at = pl.ds(pl.multiple_of((2 * c + par) * CH, CH), CH)
            ref[c, :, :DH] = dk_s[at, :].astype(ref.dtype)
            ref[c, :, DH:] = dv_s[at, :].astype(ref.dtype)


def combine_kernel(meta, p0, p1, p2, p3, s0, s1, s2, s3, out_ref):
    x = meta[0]
    for r in range(NG):
        lanes = slice(r * L, (r + 1) * L)
        _, _, parts = merged([st[x, :, lanes] for st in (s0, s1, s2, s3)])
        out = sum(p[:, lanes].astype(F32) * w for p, w in zip((p0, p1, p2, p3), parts))
        for h in range(HH):
            out_ref[r * RG : (r + 1) * RG, h * DH : (h + 1) * DH] = (
                out[:, h * RG : (h + 1) * RG].T.astype(BF)
            )


SMEM = pl.BlockSpec(memory_space=pltpu.SMEM)
VMEM = pl.BlockSpec(memory_space=pltpu.VMEM)
PARAMS = pltpu.CompilerParams(vmem_limit_bytes=48 * 1024 * 1024)
SDS = jax.ShapeDtypeStruct


def run_forward(meta, own, other, slots):
    return pl.pallas_call(
        forward_kernel,
        in_specs=[SMEM] + [VMEM] * 6,
        out_specs=[VMEM] * 2,
        out_shape=[SDS((4, DH, HH * ROWS), BF), SDS((4, 3, HH * ROWS), F32)],
        scratch_shapes=[
            pltpu.VMEM((4, 2 * ROWS, HH * DH), BF),
            pltpu.VMEM(((NB + PAD) * CH, DH), BF),
            pltpu.VMEM((DH, (NB + PAD) * CH), BF),
            pltpu.VMEM((DH, L), F32),
            pltpu.VMEM((1, L), F32),
            pltpu.VMEM((1, L), F32),
        ],
        compiler_params=PARAMS,
        name="forward",
    )(meta, own, other, *slots)


def run_backward(meta, own, other, slots, stats):
    return pl.pallas_call(
        backward_kernel,
        in_specs=[SMEM] + [VMEM] * 10,
        out_specs=[VMEM] * 3,
        out_shape=[
            SDS((4, ROWS, HH * DH), BF),
            SDS((NB // 2, CH, 2 * DH), F32),
            SDS((NB // 2, CH, 2 * DH), BF),
        ],
        scratch_shapes=[
            pltpu.VMEM((4, 2 * ROWS, HH * DH), BF),
            pltpu.VMEM(((NB + PAD) * CH, DH), BF),
            pltpu.VMEM(((NB + PAD) * CH, DH), BF),
            pltpu.VMEM((DH, (NB + PAD) * CH), BF),
            pltpu.VMEM(((NB + PAD) * CH, DH), F32),
            pltpu.VMEM(((NB + PAD) * CH, DH), F32),
            pltpu.VMEM((DH, L), F32),
        ],
        compiler_params=PARAMS,
        name="backward",
    )(meta, own, other, *slots, *stats)


def run_combine(meta, pieces, stats):
    return pl.pallas_call(
        combine_kernel,
        in_specs=[SMEM] + [VMEM] * 8,
        out_specs=VMEM,
        out_shape=SDS((ROWS, HH * DH), BF),
        compiler_params=PARAMS,
        name="combine",
    )(meta, *pieces, *stats)


def shift(value, axis, by):
    return lax.ppermute(value, axis, [(i, (i + by) % 4) for i in range(4)])


def swap(value):
    return lax.ppermute(value, "core", [(0, 1), (1, 0)])


def gathered(value, axis):
    return [value] + [shift(value, axis, by) for by in SLOT[1:]]


def local(queries, keys, values, doc_ids, out_grad):
    x, y, core = (lax.axis_index(a) for a in ("x", "y", "core"))
    meta = jnp.stack([x, y, core]).astype(jnp.int32)
    slots = gathered(jnp.concatenate([queries, out_grad], axis=0), "x")
    kv = jnp.concatenate([keys, values], axis=1).reshape(4, CH, 2 * DH)
    docs = jnp.pad(
        doc_ids.astype(BF).reshape(1, 2, 2 * DH),
        ((0, 0), (0, 14), (0, 0)),
        constant_values=3,
    )
    send = jnp.concatenate([kv, jnp.broadcast_to(docs, (4, 16, 2 * DH))], axis=1)
    send = jnp.broadcast_to(send[:, None], (4, 4, CH + 16, 2 * DH))
    own = lax.all_to_all(send.reshape(16, CH + 16, 2 * DH), XY, 0, 0)
    other = swap(own)
    ot, st = run_forward(meta, own, other, slots)
    stats = gathered(st, "x")
    pieces = [ot[0]] + [shift(ot[s], "x", 4 - SLOT[s]) for s in (1, 2, 3)]
    dq, mine, theirs = run_backward(meta, own, other, slots, stats)
    attn_out = run_combine(meta, pieces, [stats[0], stats[2], stats[1], stats[3]])
    dqs = [dq[0]] + [shift(dq[s], "x", 4 - SLOT[s]) for s in (1, 2, 3)]
    terms = (mine + swap(theirs).astype(F32)).astype(BF)
    back = lax.all_to_all(terms, XY, 0, 0).reshape(4, 4, CH, 2 * DH)
    part = jnp.sum(back.astype(F32), axis=1).astype(BF)
    cut = lax.all_to_all(part, "z", 0, 0)
    mineonly = jnp.sum(cut.astype(F32), axis=0).astype(BF)
    every = gathered(mineonly, "z")
    z = lax.axis_index("z")
    whole = jnp.zeros((4, CH, 2 * DH), BF)
    for s, piece in enumerate(every):
        whole = lax.dynamic_update_index_in_dim(whole, piece, (z - SLOT[s]) % 4, 0)
    whole = whole.astype(F32).reshape(ROWS, 2 * DH)
    scale = DH**-0.5
    q_grad = sum(d.astype(F32) for d in dqs) * scale
    return attn_out, q_grad, whole[:, :DH] * scale, whole[:, DH:]


def solution(mesh):
    fine = Mesh(mesh.devices.reshape(4, 4, 2, 4), ("x", "y", "core", "z"))
    ctx = ("x", "y", "core")
    return jax.shard_map(
        local,
        mesh=fine,
        in_specs=(P(ctx, "z"), P(ctx, None), P(ctx, None), P(ctx), P(ctx, "z")),
        out_specs=(P(ctx, "z"), P(ctx, "z"), P(ctx, None), P(ctx, None)),
        check_vma=False,
    )
```

```python
import functools
import math

import jax
import jax.numpy as jnp
from jax import lax
from jax.experimental import pallas as pl
from jax.experimental.pallas import tpu as pltpu
from jax.sharding import Mesh, PartitionSpec as P

BF = jnp.bfloat16
F32 = jnp.float32
DH = 128
ROWS = 512
CH = 128
NB = 32
HH = 2
RG = 256
NG = ROWS // RG
L = HH * RG
TF = 4
TB = 2
PAD = 4
SLOT = (0, 1, 3, 2)
LOW = -1e30
COEF = DH**-0.5 * math.log2(math.e)


def pieces_of(refs):
    for far in (0, 1):
        for n in range(5):
            ref, t = refs[5 * far + n], min(n, 3)
            first = 2 if n == 4 else 0
            for s in range(first, first + ref.shape[0] // (CH + 16)):
                yield ref, (s - first) * (CH + 16), s, t, far


def chunk_at(meta, s, t, far):
    x, y, core = meta[0], meta[1], meta[2]
    xb, yb = (x - SLOT[s] + 4) % 4, (y - SLOT[t] + 4) % 4
    par = 1 - core if far else core
    return pl.multiple_of((2 * (4 * xb + yb) + par) * CH, CH)


def load_keys(refs, meta, k_s, v_s, kt_s, vt_s):
    for ref, first, s, t, far in pieces_of(refs):
        at = chunk_at(meta, s, t, far)
        kc = ref[first : first + CH, :DH]
        vc = ref[first : first + CH, DH:]
        k_s[pl.ds(at, CH), :] = kc
        if v_s is not None:
            v_s[pl.ds(at, CH), :] = vc
        if kt_s is not None:
            kt_s[:, pl.ds(at, CH)] = kc.T
        if vt_s is not None:
            vt_s[:, pl.ds(at, CH)] = vc.T
    tail = NB * CH
    k_s[tail:, :] = jnp.zeros((PAD * CH, DH), BF)
    if v_s is not None:
        v_s[tail:, :] = jnp.zeros((PAD * CH, DH), BF)
    if kt_s is not None:
        kt_s[:, tail:] = jnp.zeros((DH, PAD * CH), BF)
    if vt_s is not None:
        vt_s[:, tail:] = jnp.zeros((DH, PAD * CH), BF)


def doc_starts(refs):
    docs = jnp.concatenate(
        [ref[first + CH : first + CH + 16, :] for ref, first, _, _, _ in pieces_of(refs)], axis=0
    ).astype(F32)
    return [jnp.sum(jnp.where(docs < d, 1.0, 0.0)).astype(jnp.int32) for d in (1, 2, 3)]


def start_of(pos, starts):
    begin = jnp.zeros_like(pos)
    for c in starts:
        begin = jnp.where(pos >= c, c, begin)
    return begin


def group_facts(meta, gi, starts, step):
    x, y, core = meta[0], meta[1], meta[2]
    slot = gi // NG
    r = gi % NG
    back = jnp.where(slot == 2, 3, jnp.where(slot == 3, 2, slot))
    xs = (x - back + 4) % 4
    row0 = (8 * xs + 2 * y + core) * ROWS + r * RG
    lane = lax.broadcasted_iota(jnp.int32, (1, L), 1)
    rpos = row0 + lane % RG
    ds = start_of(rpos, starts)
    ds_min = start_of(row0, starts)
    ds_max = start_of(row0 + RG - 1, starts)
    lo = (ds_min - CH * x + (ROWS - CH)) // ROWS
    end = (row0 + RG - 1 - CH * x + ROWS) // ROWS
    tiles = jnp.maximum(0, (end - lo + step - 1) // step)
    return slot, r, xs, row0, rpos, ds, ds_max, lo, tiles


def load_rows(rows_s, refs):
    for s in range(3):
        rows_s[s] = refs[s][...]
    rows_s[3, : ROWS // 2] = refs[3][...]
    rows_s[3, ROWS // 2 :] = refs[4][...]


def group_rows(ref, slot, r):
    at = pl.multiple_of(r * RG, RG)
    both = ref[slot, pl.ds(at, RG), :]
    return both[:, :DH], both[:, DH:]


def keep_of(m0, x, rpos, ds, step):
    base = m0 * ROWS + x * CH
    i = lax.broadcasted_iota(jnp.int32, (step * CH, 1), 0)
    kpos = base + i + (ROWS - CH) * (i // CH)
    return (kpos <= rpos) & (kpos >= ds)


def mm(a, b):
    return jnp.dot(a, b, preferred_element_type=F32)


def forward_kernel(
    meta, n0, n1, n2, n3, n4, f0, f1, f2, f3, f4, a0, a1, a2, b1, b2,
    ot0, ot1, ot2, ot3, st_ref, q_s, k_s, vt_s, acc_s, m_s, l_s, ot_s,
):
    x = meta[0]
    refs = (n0, n1, n2, n3, n4, f0, f1, f2, f3, f4)
    load_rows(q_s, (a0, a1, a2, b1, b2))
    load_keys(refs, meta, k_s, None, None, vt_s)
    starts = doc_starts(refs)

    def group(gi, carry):
        slot, r, xs, row0, rpos, ds, ds_max, lo, tiles = group_facts(meta, gi, starts, TF)
        q0, q1 = group_rows(q_s, slot, r)
        qt = jnp.concatenate([q0.T, q1.T], axis=1)
        acc_s[...] = jnp.zeros_like(acc_s)
        m_s[...] = jnp.full_like(m_s, LOW)
        l_s[...] = jnp.zeros_like(l_s)

        def tile(i, carry):
            m0 = lo + i * TF
            at = pl.multiple_of(m0 * CH, CH)

            def work(masked):
                kt = k_s[pl.ds(at, TF * CH), :]
                s = mm(kt, qt)
                if masked:
                    keep = keep_of(m0, x, rpos, ds, TF)
                    s = jnp.where(keep, s, LOW)
                m_old = m_s[...]
                m_new = jnp.maximum(m_old, jnp.max(s, axis=0, keepdims=True) * COEF)
                alpha = jnp.exp2(m_old - m_new)
                p = jnp.exp2(s * COEF - m_new)
                if masked:
                    p = jnp.where(keep, p, 0.0)
                l_s[...] = l_s[...] * alpha + jnp.sum(p, axis=0, keepdims=True)
                m_s[...] = m_new
                acc_s[...] = acc_s[...] * alpha + mm(vt_s[:, pl.ds(at, TF * CH)], p.astype(BF))

            whole = ((m0 + TF - 1) * ROWS + x * CH + CH - 1 <= row0) & (
                m0 * ROWS + x * CH >= ds_max
            )
            pl.when(whole)(functools.partial(work, False))
            pl.when(jnp.logical_not(whole))(functools.partial(work, True))
            return carry

        lax.fori_loop(0, tiles, tile, 0)
        acc = acc_s[...]
        l = l_s[...]
        lanes = pl.ds(pl.multiple_of(r * L, L), L)
        ot_s[slot, :, lanes] = (acc / jnp.where(l > 0, l, 1.0)).astype(BF)
        st_ref[xs, 0:1, lanes] = m_s[...]
        st_ref[xs, 1:2, lanes] = l
        return carry

    lax.fori_loop(0, 4 * NG, group, 0)
    for slot, ref in enumerate((ot0, ot1, ot2, ot3)):
        ref[...] = ot_s[slot]


def delta_kernel(
    meta, a0, a1, a2, b1, b2, ot0, ot1, ot2, ot3, ml_ref, st_ref, g_s
):
    x = meta[0]
    ots = (ot0, ot1, ot2, ot3)
    load_rows(g_s, (a0, a1, a2, b1, b2))
    for slot in range(4):
        xs = (x - SLOT[slot] + 4) % 4
        for r in range(NG):
            lanes = slice(r * L, (r + 1) * L)
            g0, g1 = group_rows(g_s, slot, r)
            gt = jnp.concatenate([g0.T, g1.T], axis=1).astype(F32)
            l = ml_ref[xs, 1:2, lanes]
            part = jnp.sum(ots[slot][:, lanes].astype(F32) * gt, axis=0, keepdims=True)
            st_ref[xs, 0:2, lanes] = ml_ref[xs, :, lanes]
            st_ref[xs, 2:3, lanes] = part * l


def merged(sts):
    top = functools.reduce(jnp.maximum, [st[0:1] for st in sts])
    scale = [jnp.exp2(st[0:1] - top) for st in sts]
    total = sum(st[1:2] * f for st, f in zip(sts, scale))
    delta = sum(st[2:3] * f for st, f in zip(sts, scale)) / total
    parts = [st[1:2] * f / total for st, f in zip(sts, scale)]
    return top + jnp.log2(total), delta, parts


def backward_kernel(
    meta, n0, n1, n2, n3, n4, f0, f1, f2, f3, f4, a0, a1, a2, b1, b2, c0, c1, c2, d1, d2,
    s0, s1, s2, s3, dq0, dq1, dq2, dq3, mine_ref, theirs_ref,
    q_s, g_s, k_s, v_s, kt_s, dk_s, dv_s, acc_s, dq_s,
):
    x = meta[0]
    refs = (n0, n1, n2, n3, n4, f0, f1, f2, f3, f4)
    load_rows(q_s, (a0, a1, a2, b1, b2))
    load_rows(g_s, (c0, c1, c2, d1, d2))
    load_keys(refs, meta, k_s, v_s, kt_s, None)
    starts = doc_starts(refs)
    dk_s[...] = jnp.zeros_like(dk_s)
    dv_s[...] = jnp.zeros_like(dv_s)

    def group(gi, carry):
        slot, r, xs, row0, rpos, ds, ds_max, lo, tiles = group_facts(meta, gi, starts, TB)
        q0, q1 = group_rows(q_s, slot, r)
        g0, g1 = group_rows(g_s, slot, r)
        qt = jnp.concatenate([q0.T, q1.T], axis=1)
        gt = jnp.concatenate([g0.T, g1.T], axis=1)
        qm = jnp.concatenate([q0, q1], axis=0)
        gm = jnp.concatenate([g0, g1], axis=0)
        lanes = pl.ds(pl.multiple_of(r * L, L), L)
        lse, delta, _ = merged([st[xs, :, lanes] for st in (s0, s1, s2, s3)])
        acc_s[...] = jnp.zeros_like(acc_s)

        def tile(i, carry):
            m0 = lo + i * TB
            at = pl.multiple_of(m0 * CH, CH)
            here = pl.ds(at, TB * CH)

            def work(masked):
                s = mm(k_s[here, :], qt)
                p = jnp.exp2(s * COEF - lse)
                if masked:
                    p = jnp.where(keep_of(m0, x, rpos, ds, TB), p, 0.0)
                dp = mm(v_s[here, :], gt)
                dsc = (p * (dp - delta)).astype(BF)
                dv_s[here, :] += mm(p.astype(BF), gm)
                dk_s[here, :] += mm(dsc, qm)
                acc_s[...] += mm(kt_s[:, here], dsc)

            whole = ((m0 + TB - 1) * ROWS + x * CH + CH - 1 <= row0) & (
                m0 * ROWS + x * CH >= ds_max
            )
            pl.when(whole)(functools.partial(work, False))
            pl.when(jnp.logical_not(whole))(functools.partial(work, True))
            return carry

        lax.fori_loop(0, tiles, tile, 0)
        acc = acc_s[...]
        rows_at = pl.ds(pl.multiple_of(r * RG, RG), RG)
        for h in range(HH):
            part = acc[:, h * RG : (h + 1) * RG].T
            dq_s[slot, rows_at, h * DH : (h + 1) * DH] = part.astype(BF)
        return carry

    lax.fori_loop(0, 4 * NG, group, 0)
    for slot, ref in enumerate((dq0, dq1, dq2, dq3)):
        ref[...] = dq_s[slot]
    for t in range(4):
        for s in range(4):
            for far, ref in ((0, mine_ref), (1, theirs_ref)):
                at = pl.ds(chunk_at(meta, s, t, far), CH)
                ref[t, s, :, :DH] = dk_s[at, :].astype(BF)
                ref[t, s, :, DH:] = dv_s[at, :].astype(BF)


def join_kernel(mine_ref, theirs_ref, *outs):
    for t, ref in enumerate(outs):
        ref[...] = (mine_ref[t].astype(F32) + theirs_ref[t].astype(F32)).astype(BF)


def sum_kernel(p0, p1, p2, p3, out_ref):
    out_ref[...] = sum(p[...].astype(F32) for p in (p0, p1, p2, p3)).astype(BF)


def part_kernel(p0, p1, p2, p3, *outs):
    for s, ref in enumerate(outs):
        ref[...] = sum(p[s].astype(F32) for p in (p0, p1, p2, p3)).astype(BF)


def place_kernel(meta, p0, p1, p2, p3, dk_ref, dv_ref):
    for s, ref in enumerate((p0, p1, p2, p3)):
        at = pl.ds(pl.multiple_of((meta[0] + SLOT[s]) % 4 * CH, CH), CH)
        dk_ref[at, :] = ref[:, :DH].astype(F32) * DH**-0.5
        dv_ref[at, :] = ref[:, DH:].astype(F32)


def query_kernel(p0, p1, p2, p3, out_ref):
    out_ref[...] = sum(p[...].astype(F32) for p in (p0, p1, p2, p3)) * DH**-0.5


def combine_kernel(meta, p0, p1, p2, p3, s0, s1, s2, s3, out_ref):
    x = meta[0]
    for r in range(NG):
        lanes = slice(r * L, (r + 1) * L)
        _, _, parts = merged([st[x, :, lanes] for st in (s0, s1, s2, s3)])
        out = sum(p[:, lanes].astype(F32) * w for p, w in zip((p0, p1, p2, p3), parts))
        for h in range(HH):
            out_ref[r * RG : (r + 1) * RG, h * DH : (h + 1) * DH] = (
                out[:, h * RG : (h + 1) * RG].T.astype(BF)
            )


SMEM = pl.BlockSpec(memory_space=pltpu.SMEM)
VMEM = pl.BlockSpec(memory_space=pltpu.VMEM)
PARAMS = pltpu.CompilerParams(vmem_limit_bytes=48 * 1024 * 1024)
SDS = jax.ShapeDtypeStruct


def cost(us, size):
    return pl.CostEstimate(flops=us * 10**9, bytes_accessed=size, transcendentals=0)


def call(kernel, name, us, n_in, outs, scratch=(), smem=True):
    return pl.pallas_call(
        kernel,
        in_specs=[SMEM] * smem + [VMEM] * n_in,
        out_specs=[VMEM] * len(outs),
        out_shape=outs,
        scratch_shapes=list(scratch),
        compiler_params=PARAMS,
        cost_estimate=cost(us, 1 << 20),
        name=name,
    )


ROWS_S = pltpu.VMEM((4, ROWS, HH * DH), BF)
KEYS_S = pltpu.VMEM(((NB + PAD) * CH, DH), BF)
TURN_S = pltpu.VMEM((DH, (NB + PAD) * CH), BF)
GRAD_S = pltpu.VMEM(((NB + PAD) * CH, DH), F32)
ACC_S = pltpu.VMEM((DH, L), F32)
LINE_S = pltpu.VMEM((1, L), F32)


def run_forward(meta, keys, slots):
    *ots, ml = call(
        forward_kernel,
        "forward",
        20,
        15,
        [SDS((DH, HH * ROWS), BF)] * 4 + [SDS((4, 2, HH * ROWS), F32)],
        [ROWS_S, KEYS_S, TURN_S, ACC_S, LINE_S, LINE_S, pltpu.VMEM((4, DH, HH * ROWS), BF)],
    )(meta, *keys, *slots)
    return ots, ml


def run_delta(meta, slots, ots, ml):
    return call(delta_kernel, "delta", 2, 10, [SDS((4, 3, HH * ROWS), F32)], [ROWS_S])(
        meta, *slots, *ots, ml
    )[0]


def run_backward(meta, keys, qslots, gslots, stats):
    *dqs, mine, theirs = call(
        backward_kernel,
        "backward",
        25,
        24,
        [SDS((ROWS, HH * DH), BF)] * 4 + [SDS((4, 4, CH, 2 * DH), BF)] * 2,
        [ROWS_S, ROWS_S, KEYS_S, KEYS_S, TURN_S, GRAD_S, GRAD_S, ACC_S, ROWS_S],
    )(meta, *keys, *qslots, *gslots, *stats)
    return dqs, mine, theirs


def run_combine(meta, pieces, stats):
    return call(combine_kernel, "combine", 1, 8, [SDS((ROWS, HH * DH), BF)])(
        meta, *pieces, *stats
    )[0]


def shift(value, axis, by):
    return lax.ppermute(value, axis, [(i, (i + by) % 4) for i in range(4)])


def swap(value):
    return lax.ppermute(value, "core", [(0, 1), (1, 0)])


def gathered(value, axis):
    return [value] + [shift(value, axis, by) for by in SLOT[1:]]


def ring(value, axis):
    half = value.shape[0] // 2
    one, two = shift(value, axis, 1), shift(value, axis, 3)
    return [value, one, two, shift(one[:half], axis, 1), shift(two[half:], axis, 3)]


def sent_back(slots, axis):
    return [slots[0]] + [shift(slots[s], axis, 4 - SLOT[s]) for s in (1, 2, 3)]


def local(queries, keys, values, doc_ids, out_grad):
    x, y, core = (lax.axis_index(a) for a in ("x", "y", "core"))
    meta = jnp.stack([x, y, core]).astype(jnp.int32)
    kv = jnp.concatenate([keys, values], axis=1).reshape(4, CH, 2 * DH)
    docs = jnp.pad(
        doc_ids.astype(BF).reshape(1, 2, 2 * DH),
        ((0, 0), (0, 14), (0, 0)),
        constant_values=3,
    )
    kv = jnp.concatenate([kv, jnp.broadcast_to(docs, (4, 16, 2 * DH))], axis=1)
    chunks = [lax.dynamic_index_in_dim(kv, (x + k) % 4, 0, keepdims=False) for k in SLOT]
    column = jnp.concatenate([chunks[0]] + [shift(chunks[s], "x", SLOT[s]) for s in (1, 2, 3)])
    near = ring(column, "y")
    keys_all = near + [swap(n) for n in near]
    qslots = ring(queries, "x")
    gslots = ring(out_grad, "x")
    ots, ml = run_forward(meta, keys_all, qslots)
    stats = gathered(run_delta(meta, gslots, ots, ml), "x")
    pieces = sent_back(ots, "x")
    dqs, mine, theirs = run_backward(meta, keys_all, qslots, gslots, stats)
    attn_out = run_combine(meta, pieces, [stats[0], stats[2], stats[1], stats[3]])
    column = SDS((4, CH, 2 * DH), BF)
    chunk = SDS((CH, 2 * DH), BF)
    terms = call(join_kernel, "join", 1, 2, [column] * 4, smem=False)(mine, swap(theirs))
    summed = call(sum_kernel, "sum", 1, 4, [column], smem=False)(*sent_back(terms, "y"))[0]
    parts = call(part_kernel, "part", 1, 4, [chunk] * 4, smem=False)(*gathered(summed, "z"))
    k_grad, v_grad = call(place_kernel, "place", 1, 4, [SDS((ROWS, DH), F32)] * 2)(
        meta, *sent_back(parts, "x")
    )
    q_grad = call(query_kernel, "query", 1, 4, [SDS((ROWS, HH * DH), F32)], smem=False)(
        *sent_back(dqs, "x")
    )[0]
    return attn_out, q_grad, k_grad, v_grad


def solution(mesh):
    fine = Mesh(mesh.devices.reshape(4, 4, 2, 4), ("x", "y", "core", "z"))
    ctx = ("x", "y", "core")
    return jax.shard_map(
        local,
        mesh=fine,
        in_specs=(P(ctx, "z"), P(ctx, None), P(ctx, None), P(ctx), P(ctx, "z")),
        out_specs=(P(ctx, "z"), P(ctx, "z"), P(ctx, None), P(ctx, None)),
        check_vma=False,
    )
```

```python
import functools
import math

import jax
import jax.numpy as jnp
from jax import lax
from jax.experimental import pallas as pl
from jax.experimental.pallas import tpu as pltpu
from jax.sharding import Mesh, PartitionSpec as P

BF = jnp.bfloat16
F32 = jnp.float32
DH = 128
ROWS = 512
CH = 128
NB = 32
HH = 2
RG = 512
NG = ROWS // RG
L = HH * RG
TF = 8
TB = 8
PAD = 8
SLOT = (0, 1, 3, 2)
LOW = -1e30
COEF = DH**-0.5 * math.log2(math.e)


def pieces_of(refs):
    for far in (0, 1):
        for t in range(4):
            for s in range(4):
                yield refs[4 * far + t], s * (CH + 16), s, t, far


def chunk_at(meta, s, t, far):
    x, y, core = meta[0], meta[1], meta[2]
    xb, yb = (x - SLOT[s] + 4) % 4, (y - SLOT[t] + 4) % 4
    par = 1 - core if far else core
    return pl.multiple_of((2 * (4 * xb + yb) + par) * CH, CH)


def load_keys(refs, meta, k_s, v_s, kt_s, vt_s):
    for ref, first, s, t, far in pieces_of(refs):
        at = chunk_at(meta, s, t, far)
        kc = ref[first : first + CH, :DH]
        vc = ref[first : first + CH, DH:]
        k_s[pl.ds(at, CH), :] = kc
        if v_s is not None:
            v_s[pl.ds(at, CH), :] = vc
        if kt_s is not None:
            kt_s[:, pl.ds(at, CH)] = kc.T
        if vt_s is not None:
            vt_s[:, pl.ds(at, CH)] = vc.T
    tail = NB * CH
    k_s[tail:, :] = jnp.zeros((PAD * CH, DH), BF)
    if v_s is not None:
        v_s[tail:, :] = jnp.zeros((PAD * CH, DH), BF)
    if kt_s is not None:
        kt_s[:, tail:] = jnp.zeros((DH, PAD * CH), BF)
    if vt_s is not None:
        vt_s[:, tail:] = jnp.zeros((DH, PAD * CH), BF)


def doc_starts(refs):
    docs = jnp.concatenate(
        [ref[first + CH : first + CH + 16, :] for ref, first, _, _, _ in pieces_of(refs)], axis=0
    ).astype(F32)
    return [jnp.sum(jnp.where(docs < d, 1.0, 0.0)).astype(jnp.int32) for d in (1, 2, 3)]


def start_of(pos, starts):
    begin = jnp.zeros_like(pos)
    for c in starts:
        begin = jnp.where(pos >= c, c, begin)
    return begin


def group_facts(meta, gi, starts, step):
    x, y, core = meta[0], meta[1], meta[2]
    slot = gi // NG
    r = gi % NG
    back = jnp.where(slot == 2, 3, jnp.where(slot == 3, 2, slot))
    xs = (x - back + 4) % 4
    row0 = (8 * xs + 2 * y + core) * ROWS + r * RG
    lane = lax.broadcasted_iota(jnp.int32, (1, L), 1)
    rpos = row0 + lane % RG
    ds = start_of(rpos, starts)
    ds_min = start_of(row0, starts)
    ds_max = start_of(row0 + RG - 1, starts)
    lo = (ds_min - CH * x + (ROWS - CH)) // ROWS
    end = (row0 + RG - 1 - CH * x + ROWS) // ROWS
    tiles = jnp.maximum(0, (end - lo + step - 1) // step)
    return slot, r, xs, row0, rpos, ds, ds_max, lo, tiles


def load_rows(rows_s, refs):
    for s, ref in enumerate(refs):
        rows_s[s] = ref[...]


def group_rows(ref, slot, r):
    at = pl.multiple_of(r * RG, RG)
    both = ref[slot, pl.ds(at, RG), :]
    return both[:, :DH], both[:, DH:]


def keep_of(m0, x, rpos, ds, step):
    base = m0 * ROWS + x * CH
    i = lax.broadcasted_iota(jnp.int32, (step * CH, 1), 0)
    kpos = base + i + (ROWS - CH) * (i // CH)
    return (kpos <= rpos) & (kpos >= ds)


def is_whole(m0, x, row0, ds_max, step):
    first = m0 * ROWS + x * CH
    return (first + (step - 1) * ROWS + CH - 1 <= row0) & (first >= ds_max)


def mm(a, b):
    return jnp.dot(a, b, preferred_element_type=F32)


def forward_kernel(
    meta, n0, n1, n2, n3, f0, f1, f2, f3, a0, a1, a2, a3,
    ot0, ot1, ot2, ot3, st_ref, q_s, k_s, vt_s, acc_s, m_s, l_s, ot_s,
):
    x = meta[0]
    refs = (n0, n1, n2, n3, f0, f1, f2, f3)
    load_rows(q_s, (a0, a1, a2, a3))
    load_keys(refs, meta, k_s, None, None, vt_s)
    starts = doc_starts(refs)

    def group(gi, carry):
        slot, r, xs, row0, rpos, ds, ds_max, lo, tiles = group_facts(meta, gi, starts, TF)
        q0, q1 = group_rows(q_s, slot, r)
        qt = jnp.concatenate([q0.T, q1.T], axis=1)
        acc_s[...] = jnp.zeros_like(acc_s)
        m_s[...] = jnp.zeros_like(m_s)
        l_s[...] = jnp.zeros_like(l_s)

        def tile(i, carry):
            m0 = lo + i * TF
            here = pl.ds(pl.multiple_of(m0 * CH, CH), TF * CH)

            def work(masked):
                p = jnp.exp2(mm(k_s[here, :], qt) * COEF)
                if masked:
                    p = jnp.where(keep_of(m0, x, rpos, ds, TF), p, 0.0)
                l_s[...] += jnp.sum(p, axis=0, keepdims=True)
                acc_s[...] += mm(vt_s[:, here], p.astype(BF))

            whole = is_whole(m0, x, row0, ds_max, TF)
            pl.when(whole)(functools.partial(work, False))
            pl.when(jnp.logical_not(whole))(functools.partial(work, True))
            return carry

        lax.fori_loop(0, tiles, tile, 0)

        def careful_tile(i, carry):
            m0 = lo + i * TF
            here = pl.ds(pl.multiple_of(m0 * CH, CH), TF * CH)
            keep = keep_of(m0, x, rpos, ds, TF)
            s = jnp.where(keep, mm(k_s[here, :], qt), LOW)
            m_old = m_s[...]
            m_new = jnp.maximum(m_old, jnp.max(s, axis=0, keepdims=True) * COEF)
            alpha = jnp.exp2(m_old - m_new)
            p = jnp.where(keep, jnp.exp2(s * COEF - m_new), 0.0)
            l_s[...] = l_s[...] * alpha + jnp.sum(p, axis=0, keepdims=True)
            m_s[...] = m_new
            acc_s[...] = acc_s[...] * alpha + mm(vt_s[:, here], p.astype(BF))
            return carry

        block = (rpos - CH * x) >> 9
        last = jnp.minimum(rpos, block * ROWS + CH * x + CH - 1)
        some = (block >= 0) & (last >= ds)
        l = l_s[...]
        good = (jnp.min(jnp.where(some, l, 1.0)) >= 2.0**-60) & (jnp.max(l) <= 2.0**60)

        @pl.when(jnp.logical_not(good))
        def careful():
            acc_s[...] = jnp.zeros_like(acc_s)
            m_s[...] = jnp.full_like(m_s, LOW)
            l_s[...] = jnp.zeros_like(l_s)
            lax.fori_loop(0, tiles, careful_tile, 0)

        acc = acc_s[...]
        l = l_s[...]
        lanes = pl.ds(pl.multiple_of(r * L, L), L)
        ot_s[slot, :, lanes] = (acc / jnp.where(l > 0, l, 1.0)).astype(BF)
        st_ref[xs, 0:1, lanes] = m_s[...]
        st_ref[xs, 1:2, lanes] = l
        return carry

    lax.fori_loop(0, 4 * NG, group, 0)
    for slot, ref in enumerate((ot0, ot1, ot2, ot3)):
        ref[...] = ot_s[slot]


def delta_kernel(
    meta, a0, a1, a2, a3, ot0, ot1, ot2, ot3, ml_ref, st_ref, g_s
):
    x = meta[0]
    ots = (ot0, ot1, ot2, ot3)
    load_rows(g_s, (a0, a1, a2, a3))
    for slot in range(4):
        xs = (x - SLOT[slot] + 4) % 4
        for r in range(NG):
            lanes = slice(r * L, (r + 1) * L)
            g0, g1 = group_rows(g_s, slot, r)
            gt = jnp.concatenate([g0.T, g1.T], axis=1).astype(F32)
            l = ml_ref[xs, 1:2, lanes]
            part = jnp.sum(ots[slot][:, lanes].astype(F32) * gt, axis=0, keepdims=True)
            st_ref[xs, 0:2, lanes] = ml_ref[xs, :, lanes]
            st_ref[xs, 2:3, lanes] = part * l


def merged(sts):
    top = functools.reduce(jnp.maximum, [st[0:1] for st in sts])
    scale = [jnp.exp2(st[0:1] - top) for st in sts]
    total = sum(st[1:2] * f for st, f in zip(sts, scale))
    delta = sum(st[2:3] * f for st, f in zip(sts, scale)) / total
    parts = [st[1:2] * f / total for st, f in zip(sts, scale)]
    return top + jnp.log2(total), delta, parts


def backward_kernel(
    meta, n0, n1, n2, n3, f0, f1, f2, f3, a0, a1, a2, a3, c0, c1, c2, c3,
    s0, s1, s2, s3, dq0, dq1, dq2, dq3, mine_ref, theirs_ref,
    q_s, g_s, k_s, v_s, kt_s, dk_s, dv_s, acc_s, dq_s,
):
    x = meta[0]
    refs = (n0, n1, n2, n3, f0, f1, f2, f3)
    load_rows(q_s, (a0, a1, a2, a3))
    load_rows(g_s, (c0, c1, c2, c3))
    load_keys(refs, meta, k_s, v_s, kt_s, None)
    starts = doc_starts(refs)
    dk_s[...] = jnp.zeros_like(dk_s)
    dv_s[...] = jnp.zeros_like(dv_s)

    def group(gi, carry):
        slot, r, xs, row0, rpos, ds, ds_max, lo, tiles = group_facts(meta, gi, starts, TB)
        q0, q1 = group_rows(q_s, slot, r)
        g0, g1 = group_rows(g_s, slot, r)
        qt = jnp.concatenate([q0.T, q1.T], axis=1)
        gt = jnp.concatenate([g0.T, g1.T], axis=1)
        qm = jnp.concatenate([q0, q1], axis=0)
        gm = jnp.concatenate([g0, g1], axis=0)
        lanes = pl.ds(pl.multiple_of(r * L, L), L)
        lse, delta, _ = merged([st[xs, :, lanes] for st in (s0, s1, s2, s3)])
        acc_s[...] = jnp.zeros_like(acc_s)

        def tile(i, carry):
            m0 = lo + i * TB
            at = pl.multiple_of(m0 * CH, CH)
            here = pl.ds(at, TB * CH)

            def work(masked):
                s = mm(k_s[here, :], qt)
                p = jnp.exp2(s * COEF - lse)
                if masked:
                    p = jnp.where(keep_of(m0, x, rpos, ds, TB), p, 0.0)
                dp = mm(v_s[here, :], gt)
                dsc = (p * (dp - delta)).astype(BF)
                dv_s[here, :] += mm(p.astype(BF), gm)
                dk_s[here, :] += mm(dsc, qm)
                acc_s[...] += mm(kt_s[:, here], dsc)

            whole = is_whole(m0, x, row0, ds_max, TB)
            pl.when(whole)(functools.partial(work, False))
            pl.when(jnp.logical_not(whole))(functools.partial(work, True))
            return carry

        lax.fori_loop(0, tiles, tile, 0)
        acc = acc_s[...]
        rows_at = pl.ds(pl.multiple_of(r * RG, RG), RG)
        for h in range(HH):
            part = acc[:, h * RG : (h + 1) * RG].T
            dq_s[slot, rows_at, h * DH : (h + 1) * DH] = part.astype(BF)
        return carry

    lax.fori_loop(0, 4 * NG, group, 0)
    for slot, ref in enumerate((dq0, dq1, dq2, dq3)):
        ref[...] = dq_s[slot]
    for t in range(4):
        for s in range(4):
            for far, ref in ((0, mine_ref), (1, theirs_ref)):
                at = pl.ds(chunk_at(meta, s, t, far), CH)
                ref[t, s, :, :DH] = dk_s[at, :].astype(BF)
                ref[t, s, :, DH:] = dv_s[at, :].astype(BF)


def pack_kernel(meta, keys_ref, values_ref, docs_ref, *outs):
    rest = jnp.full((16 - ROWS // DH, DH), 3.0, F32)
    docs = jnp.concatenate([docs_ref[...].astype(F32), rest], axis=0)
    docs = jnp.concatenate([docs, jnp.full((16, DH), 3.0, F32)], axis=1).astype(BF)
    for s, ref in enumerate(outs):
        at = pl.ds(pl.multiple_of((meta[0] + SLOT[s]) % 4 * CH, CH), CH)
        ref[:CH, :DH] = keys_ref[at, :]
        ref[:CH, DH:] = values_ref[at, :]
        ref[CH:, :] = docs


def join_kernel(mine_ref, theirs_ref, *outs):
    for t, ref in enumerate(outs):
        ref[...] = (mine_ref[t].astype(F32) + theirs_ref[t].astype(F32)).astype(BF)


def sum_kernel(p0, p1, p2, p3, out_ref):
    out_ref[...] = sum(p[...].astype(F32) for p in (p0, p1, p2, p3)).astype(BF)


def split_kernel(meta, p0, p1, p2, p3, *outs):
    for k, ref in enumerate(outs):
        s = (meta[3] + SLOT[k]) % 4
        ref[...] = sum(p[s].astype(F32) for p in (p0, p1, p2, p3)).astype(BF)


def place_kernel(meta, p0, p1, p2, p3, dk_ref, dv_ref):
    for k, ref in enumerate((p0, p1, p2, p3)):
        s = (meta[3] - SLOT[k] + 4) % 4
        step = jnp.where(s == 2, 3, jnp.where(s == 3, 2, s))
        at = pl.ds(pl.multiple_of((meta[0] + step) % 4 * CH, CH), CH)
        dk_ref[at, :] = ref[:, :DH].astype(F32) * DH**-0.5
        dv_ref[at, :] = ref[:, DH:].astype(F32)


def query_kernel(p0, p1, p2, p3, out_ref):
    out_ref[...] = sum(p[...].astype(F32) for p in (p0, p1, p2, p3)) * DH**-0.5


def combine_kernel(meta, p0, p1, p2, p3, s0, s1, s2, s3, out_ref):
    x = meta[0]
    for r in range(NG):
        lanes = slice(r * L, (r + 1) * L)
        _, _, parts = merged([st[x, :, lanes] for st in (s0, s1, s2, s3)])
        out = sum(p[:, lanes].astype(F32) * w for p, w in zip((p0, p1, p2, p3), parts))
        for h in range(HH):
            out_ref[r * RG : (r + 1) * RG, h * DH : (h + 1) * DH] = (
                out[:, h * RG : (h + 1) * RG].T.astype(BF)
            )


SMEM = pl.BlockSpec(memory_space=pltpu.SMEM)
VMEM = pl.BlockSpec(memory_space=pltpu.VMEM)
PARAMS = pltpu.CompilerParams(vmem_limit_bytes=48 * 1024 * 1024)
SDS = jax.ShapeDtypeStruct


def cost(us, size):
    return pl.CostEstimate(flops=us * 10**9, bytes_accessed=size, transcendentals=0)


def call(kernel, name, us, n_in, outs, scratch=(), smem=True):
    return pl.pallas_call(
        kernel,
        in_specs=[SMEM] * smem + [VMEM] * n_in,
        out_specs=[VMEM] * len(outs),
        out_shape=outs,
        scratch_shapes=list(scratch),
        compiler_params=PARAMS,
        cost_estimate=cost(us, 1 << 20),
        name=name,
    )


ROWS_S = pltpu.VMEM((4, ROWS, HH * DH), BF)
KEYS_S = pltpu.VMEM(((NB + PAD) * CH, DH), BF)
TURN_S = pltpu.VMEM((DH, (NB + PAD) * CH), BF)
GRAD_S = pltpu.VMEM(((NB + PAD) * CH, DH), F32)
ACC_S = pltpu.VMEM((DH, L), F32)
LINE_S = pltpu.VMEM((1, L), F32)


def run_forward(meta, keys, slots):
    *ots, ml = call(
        forward_kernel,
        "forward",
        12,
        12,
        [SDS((DH, HH * ROWS), BF)] * 4 + [SDS((4, 2, HH * ROWS), F32)],
        [ROWS_S, KEYS_S, TURN_S, ACC_S, LINE_S, LINE_S, pltpu.VMEM((4, DH, HH * ROWS), BF)],
    )(meta, *keys, *slots)
    return ots, ml


def run_delta(meta, slots, ots, ml):
    return call(delta_kernel, "delta", 1, 9, [SDS((4, 3, HH * ROWS), F32)], [ROWS_S])(
        meta, *slots, *ots, ml
    )[0]


def run_backward(meta, keys, qslots, gslots, stats):
    *dqs, mine, theirs = call(
        backward_kernel,
        "backward",
        25,
        20,
        [SDS((ROWS, HH * DH), BF)] * 4 + [SDS((4, 4, CH, 2 * DH), BF)] * 2,
        [ROWS_S, ROWS_S, KEYS_S, KEYS_S, TURN_S, GRAD_S, GRAD_S, ACC_S, ROWS_S],
    )(meta, *keys, *qslots, *gslots, *stats)
    return dqs, mine, theirs


def run_combine(meta, pieces, stats):
    return call(combine_kernel, "combine", 1, 8, [SDS((ROWS, HH * DH), BF)])(
        meta, *pieces, *stats
    )[0]


def shift(value, axis, by):
    return lax.ppermute(value, axis, [(i, (i + by) % 4) for i in range(4)])


def swap(value):
    return lax.ppermute(value, "core", [(0, 1), (1, 0)])


def gathered(value, axis):
    return [value] + [shift(value, axis, by) for by in SLOT[1:]]


def sent_back(slots, axis):
    return [slots[0]] + [shift(slots[s], axis, 4 - SLOT[s]) for s in (1, 2, 3)]


def local(queries, keys, values, doc_ids, out_grad):
    meta = jnp.stack([lax.axis_index(a) for a in ("x", "y", "core", "z")]).astype(jnp.int32)
    packed = SDS((CH + 16, 2 * DH), BF)
    chunks = call(pack_kernel, "pack", 1, 3, [packed] * 4)(
        meta, keys, values, doc_ids.reshape(ROWS // DH, DH)
    )
    column = jnp.concatenate([chunks[0]] + [shift(chunks[s], "x", SLOT[s]) for s in (1, 2, 3)])
    near = gathered(column, "y")
    keys_all = near + [swap(n) for n in near]
    qslots = gathered(queries, "x")
    out_grad, *near = lax.optimization_barrier((out_grad, *near))
    gslots = gathered(out_grad, "x")
    ots, ml = run_forward(meta, keys_all, qslots)
    stats = gathered(run_delta(meta, gslots, ots, ml), "x")
    pieces = sent_back(ots, "x")
    dqs, mine, theirs = run_backward(meta, keys_all, qslots, gslots, stats)
    attn_out = run_combine(meta, pieces, [stats[0], stats[2], stats[1], stats[3]])
    column = SDS((4, CH, 2 * DH), BF)
    chunk = SDS((CH, 2 * DH), BF)
    terms = call(join_kernel, "join", 1, 2, [column] * 4, smem=False)(mine, swap(theirs))
    parts = call(split_kernel, "split", 1, 4, [chunk] * 4)(meta, *sent_back(terms, "y"))
    parts = [parts[0]] + [shift(parts[k], "z", SLOT[k]) for k in (1, 2, 3)]
    one = call(sum_kernel, "sum", 1, 4, [chunk], smem=False)(*parts)[0]
    home = [(4 * a + z, (a - SLOT[z]) % 4 * 4 + z) for a in range(4) for z in range(4)]
    one = lax.ppermute(one, ("x", "z"), home)
    k_grad, v_grad = call(place_kernel, "place", 1, 4, [SDS((ROWS, DH), F32)] * 2)(
        meta, *gathered(one, "z")
    )
    q_grad = call(query_kernel, "query", 1, 4, [SDS((ROWS, HH * DH), F32)], smem=False)(
        *sent_back(dqs, "x")
    )[0]
    return attn_out, q_grad, k_grad, v_grad


def solution(mesh):
    fine = Mesh(mesh.devices.reshape(4, 4, 2, 4), ("x", "y", "core", "z"))
    ctx = ("x", "y", "core")
    return jax.shard_map(
        local,
        mesh=fine,
        in_specs=(P(ctx, "z"), P(ctx, None), P(ctx, None), P(ctx), P(ctx, "z")),
        out_specs=(P(ctx, "z"), P(ctx, "z"), P(ctx, None), P(ctx, None)),
        check_vma=False,
    )
```

```python
import functools
import math

import jax
import jax.numpy as jnp
from jax import lax
from jax.experimental import pallas as pl
from jax.experimental.pallas import tpu as pltpu
from jax.sharding import Mesh, PartitionSpec as P

BF = jnp.bfloat16
F32 = jnp.float32
DH = 128
ROWS = 512
CH = 128
NB = 32
HH = 2
RG = 512
NG = ROWS // RG
HALF = ROWS // 2
L = HH * RG
TILE = 4
PAD = 4
SLOT = (0, 1, 3, 2)
LOW = -1e30
COEF = DH**-0.5 * math.log2(math.e)


def pieces_of(refs):
    for far in (0, 1):
        for t in range(4):
            for s in range(4):
                yield refs[4 * far + t], s * (CH + 16), s, t, far


def chunk_at(meta, s, t, far):
    x, y, core = meta[0], meta[1], meta[2]
    xb, yb = (x - SLOT[s] + 4) % 4, (y - SLOT[t] + 4) % 4
    par = 1 - core if far else core
    return pl.multiple_of((2 * (4 * xb + yb) + par) * CH, CH)


def load_keys(refs, meta, k_s, v_s, kt_s, vt_s):
    for ref, first, s, t, far in pieces_of(refs):
        at = chunk_at(meta, s, t, far)
        kc = ref[first : first + CH, :DH]
        vc = ref[first : first + CH, DH:]
        k_s[pl.ds(at, CH), :] = kc
        if v_s is not None:
            v_s[pl.ds(at, CH), :] = vc
        if kt_s is not None:
            kt_s[:, pl.ds(at, CH)] = kc.T
        if vt_s is not None:
            vt_s[:, pl.ds(at, CH)] = vc.T
    tail = NB * CH
    k_s[tail:, :] = jnp.zeros((PAD * CH, DH), BF)
    if v_s is not None:
        v_s[tail:, :] = jnp.zeros((PAD * CH, DH), BF)
    if kt_s is not None:
        kt_s[:, tail:] = jnp.zeros((DH, PAD * CH), BF)
    if vt_s is not None:
        vt_s[:, tail:] = jnp.zeros((DH, PAD * CH), BF)


def doc_starts(refs):
    docs = jnp.concatenate(
        [ref[first + CH : first + CH + 16, :] for ref, first, _, _, _ in pieces_of(refs)], axis=0
    ).astype(F32)
    return [jnp.sum(jnp.where(docs < d, 1.0, 0.0)).astype(jnp.int32) for d in (1, 2, 3)]


def start_of(pos, starts):
    begin = jnp.zeros_like(pos)
    for c in starts:
        begin = jnp.where(pos >= c, c, begin)
    return begin


def group_facts(meta, gi, starts):
    x, y, core = meta[0], meta[1], meta[2]
    slot = gi // NG
    r = gi % NG
    back = jnp.where(slot == 2, 3, jnp.where(slot == 3, 2, slot))
    xs = (x - back + 4) % 4
    row0 = (8 * xs + 2 * y + core) * ROWS + r * RG
    lane = lax.broadcasted_iota(jnp.int32, (1, L), 1)
    rpos = row0 + lane % RG
    ds = start_of(rpos, starts)
    ds_min = start_of(row0, starts)
    ds_max = start_of(row0 + RG - 1, starts)
    lo = (ds_min - CH * x + (ROWS - CH)) // ROWS
    end = (row0 + RG - 1 - CH * x + ROWS) // ROWS
    return slot, r, xs, row0, rpos, ds, ds_max, lo, jnp.maximum(0, end - lo)


def group_rows(ref, slot, which):
    at = which * HALF
    both = jnp.concatenate(
        [ref[slot, at : at + HALF, :], ref[slot, ROWS + at : ROWS + at + HALF, :]], axis=0
    )
    return both[:, :DH], both[:, DH:]


def keep_of(m0, x, rpos, ds, step):
    base = m0 * ROWS + x * CH
    i = lax.broadcasted_iota(jnp.int32, (step * CH, 1), 0)
    kpos = base + i + (ROWS - CH) * (i // CH)
    return (kpos <= rpos) & (kpos >= ds)


def is_whole(m0, x, row0, ds_max, step):
    first = m0 * ROWS + x * CH
    return (first + (step - 1) * ROWS + CH - 1 <= row0) & (first >= ds_max)


def over_tiles(lo, chunks, work):
    tiles = (chunks + 1) // TILE
    tail = chunks - tiles * TILE

    def whole(i, carry):
        work(lo + i * TILE, TILE)
        return carry

    lax.fori_loop(0, tiles, whole, 0)

    @pl.when(tail > 0)
    def rest():
        work(lo + tiles * TILE, TILE // 2)


def mm(a, b):
    return jnp.dot(a, b, preferred_element_type=F32)


def forward_kernel(
    meta, n0, n1, n2, n3, f0, f1, f2, f3, qg_s,
    ot_ref, st_ref, k_s, vt_s, acc_s, m_s, l_s,
):
    x = meta[0]
    refs = (n0, n1, n2, n3, f0, f1, f2, f3)
    load_keys(refs, meta, k_s, None, None, vt_s)
    starts = doc_starts(refs)

    def group(gi, carry):
        slot, r, xs, row0, rpos, ds, ds_max, lo, chunks = group_facts(meta, gi, starts)
        q0, q1 = group_rows(qg_s, slot, 0)
        qt = jnp.concatenate([q0.T, q1.T], axis=1)
        acc_s[...] = jnp.zeros_like(acc_s)
        m_s[...] = jnp.zeros_like(m_s)
        l_s[...] = jnp.zeros_like(l_s)

        def tile(m0, step):
            here = pl.ds(pl.multiple_of(m0 * CH, CH), step * CH)

            def work(masked):
                p = jnp.exp2(mm(k_s[here, :], qt) * COEF)
                if masked:
                    p = jnp.where(keep_of(m0, x, rpos, ds, step), p, 0.0)
                l_s[...] += jnp.sum(p, axis=0, keepdims=True)
                acc_s[...] += mm(vt_s[:, here], p.astype(BF))

            whole = is_whole(m0, x, row0, ds_max, step)
            pl.when(whole)(functools.partial(work, False))
            pl.when(jnp.logical_not(whole))(functools.partial(work, True))

        over_tiles(lo, chunks, tile)

        def careful_tile(m0, step):
            here = pl.ds(pl.multiple_of(m0 * CH, CH), step * CH)
            keep = keep_of(m0, x, rpos, ds, step)
            s = jnp.where(keep, mm(k_s[here, :], qt), LOW)
            m_old = m_s[...]
            m_new = jnp.maximum(m_old, jnp.max(s, axis=0, keepdims=True) * COEF)
            alpha = jnp.exp2(m_old - m_new)
            p = jnp.where(keep, jnp.exp2(s * COEF - m_new), 0.0)
            l_s[...] = l_s[...] * alpha + jnp.sum(p, axis=0, keepdims=True)
            m_s[...] = m_new
            acc_s[...] = acc_s[...] * alpha + mm(vt_s[:, here], p.astype(BF))

        block = (rpos - CH * x) >> 9
        last = jnp.minimum(rpos, block * ROWS + CH * x + CH - 1)
        some = (block >= 0) & (last >= ds)
        l = l_s[...]
        good = (jnp.min(jnp.where(some, l, 1.0)) >= 2.0**-60) & (jnp.max(l) <= 2.0**60)

        @pl.when(jnp.logical_not(good))
        def careful():
            acc_s[...] = jnp.zeros_like(acc_s)
            m_s[...] = jnp.full_like(m_s, LOW)
            l_s[...] = jnp.zeros_like(l_s)
            over_tiles(lo, chunks, careful_tile)

        g0, g1 = group_rows(qg_s, slot, 1)
        gt = jnp.concatenate([g0.T, g1.T], axis=1).astype(F32)
        acc = acc_s[...]
        l = l_s[...]
        lanes = pl.ds(pl.multiple_of(r * L, L), L)
        ot_ref[slot, :, lanes] = (acc / jnp.where(l > 0, l, 1.0)).astype(BF)
        st_ref[xs, 0:1, lanes] = m_s[...]
        st_ref[xs, 1:2, lanes] = l
        st_ref[xs, 2:3, lanes] = jnp.sum(acc * gt, axis=0, keepdims=True)
        return carry

    lax.fori_loop(0, 4 * NG, group, 0)


def merged(sts):
    top = functools.reduce(jnp.maximum, [st[0:1] for st in sts])
    scale = [jnp.exp2(st[0:1] - top) for st in sts]
    total = sum(st[1:2] * f for st, f in zip(sts, scale))
    delta = sum(st[2:3] * f for st, f in zip(sts, scale)) / total
    return top + jnp.log2(total), delta, sts[0][1:2] * scale[0] / total


def backward_kernel(
    meta, n0, n1, n2, n3, f0, f1, f2, f3, qg_s,
    ot_ref, s0, s1, s2, s3, e0, e1, e2, e3a, e3b, mine_ref, theirs_ref,
    k_s, v_s, kt_s, dk_s, dv_s, acc_s, back_s,
):
    x = meta[0]
    refs = (n0, n1, n2, n3, f0, f1, f2, f3)
    load_keys(refs, meta, k_s, v_s, kt_s, None)
    starts = doc_starts(refs)
    dk_s[...] = jnp.zeros_like(dk_s)
    dv_s[...] = jnp.zeros_like(dv_s)

    def group(gi, carry):
        slot, r, xs, row0, rpos, ds, ds_max, lo, chunks = group_facts(meta, gi, starts)
        q0, q1 = group_rows(qg_s, slot, 0)
        g0, g1 = group_rows(qg_s, slot, 1)
        qt = jnp.concatenate([q0.T, q1.T], axis=1)
        gt = jnp.concatenate([g0.T, g1.T], axis=1)
        qm = jnp.concatenate([q0, q1], axis=0)
        gm = jnp.concatenate([g0, g1], axis=0)
        lanes = pl.ds(pl.multiple_of(r * L, L), L)
        lse, delta, share = merged([st[xs, :, lanes] for st in (s0, s1, s2, s3)])
        acc_s[...] = jnp.zeros_like(acc_s)

        def tile(m0, step):
            here = pl.ds(pl.multiple_of(m0 * CH, CH), step * CH)

            def work(masked):
                s = mm(k_s[here, :], qt)
                p = jnp.exp2(s * COEF - lse)
                if masked:
                    p = jnp.where(keep_of(m0, x, rpos, ds, step), p, 0.0)
                dp = mm(v_s[here, :], gt)
                dsc = (p * (dp - delta)).astype(BF)
                dv_s[here, :] += mm(p.astype(BF), gm)
                dk_s[here, :] += mm(dsc, qm)
                acc_s[...] += mm(kt_s[:, here], dsc)

            whole = is_whole(m0, x, row0, ds_max, step)
            pl.when(whole)(functools.partial(work, False))
            pl.when(jnp.logical_not(whole))(functools.partial(work, True))

        over_tiles(lo, chunks, tile)
        acc = acc_s[...]
        out = ot_ref[slot, :, lanes].astype(F32) * share
        for h in range(HH):
            cols = slice(h * DH, (h + 1) * DH)
            for n in range(2):
                part = slice(h * RG + n * HALF, h * RG + (n + 1) * HALF)
                back_s[slot, (2 * n) * HALF : (2 * n + 1) * HALF, cols] = acc[:, part].T.astype(BF)
                back_s[slot, (2 * n + 1) * HALF : (2 * n + 2) * HALF, cols] = out[:, part].T.astype(BF)
        return carry

    lax.fori_loop(0, 4 * NG, group, 0)
    for slot, ref in enumerate((e0, e1, e2)):
        ref[...] = back_s[slot]
    e3a[...] = back_s[3, :ROWS]
    e3b[...] = back_s[3, ROWS:]
    for t in range(4):
        for s in range(4):
            for far, ref in ((0, mine_ref), (1, theirs_ref)):
                at = pl.ds(chunk_at(meta, s, t, far), CH)
                ref[t, s, :, :DH] = dk_s[at, :].astype(BF)
                ref[t, s, :, DH:] = dv_s[at, :].astype(BF)


def pack_kernel(meta, keys_ref, values_ref, docs_ref, *outs):
    rest = jnp.full((16 - ROWS // DH, DH), 3.0, F32)
    docs = jnp.concatenate([docs_ref[...].astype(F32), rest], axis=0)
    docs = jnp.concatenate([docs, jnp.full((16, DH), 3.0, F32)], axis=1).astype(BF)
    for s, ref in enumerate(outs):
        at = pl.ds(pl.multiple_of((meta[0] + SLOT[s]) % 4 * CH, CH), CH)
        ref[:CH, :DH] = keys_ref[at, :]
        ref[:CH, DH:] = values_ref[at, :]
        ref[CH:, :] = docs


def pair_kernel(q_ref, g_ref, out_ref):
    for n in range(2):
        here = slice(n * HALF, (n + 1) * HALF)
        out_ref[2 * n * HALF : (2 * n + 1) * HALF] = q_ref[here]
        out_ref[(2 * n + 1) * HALF : (2 * n + 2) * HALF] = g_ref[here]


def stack_kernel(p0, p1, p2, p3a, p3b, out_ref):
    for s, ref in enumerate((p0, p1, p2)):
        out_ref[s] = ref[...]
    out_ref[3, :ROWS] = p3a[...]
    out_ref[3, ROWS:] = p3b[...]


def join_kernel(mine_ref, theirs_ref, *outs):
    for t, ref in enumerate(outs):
        ref[...] = (mine_ref[t].astype(F32) + theirs_ref[t].astype(F32)).astype(BF)


def sum_kernel(p0, p1, p2, p3, out_ref):
    out_ref[...] = sum(p[...].astype(F32) for p in (p0, p1, p2, p3)).astype(BF)


def split_kernel(meta, p0, p1, p2, p3, *outs):
    for k, ref in enumerate(outs):
        s = (meta[3] + SLOT[k]) % 4
        ref[...] = sum(p[s].astype(F32) for p in (p0, p1, p2, p3)).astype(BF)


def place_kernel(meta, p0, p1, p2, p3, dk_ref, dv_ref):
    for k, ref in enumerate((p0, p1, p2, p3)):
        s = (meta[3] - SLOT[k] + 4) % 4
        step = jnp.where(s == 2, 3, jnp.where(s == 3, 2, s))
        at = pl.ds(pl.multiple_of((meta[0] + step) % 4 * CH, CH), CH)
        dk_ref[at, :] = ref[:, :DH].astype(F32) * DH**-0.5
        dv_ref[at, :] = ref[:, DH:].astype(F32)


def relay_kernel(e1, e2, ra, rb, o1, o2):
    o1[:ROWS] = (e1[:ROWS].astype(F32) + ra[...].astype(F32)).astype(BF)
    o1[ROWS:] = e1[ROWS:]
    o2[:ROWS] = e2[:ROWS]
    o2[ROWS:] = (e2[ROWS:].astype(F32) + rb[...].astype(F32)).astype(BF)


def finish_kernel(p0, p1, p2, out_ref, dq_ref):
    for n in range(2):
        here = slice(n * HALF, (n + 1) * HALF)
        for k, ref in ((0, dq_ref), (1, out_ref)):
            at = slice((2 * n + k) * HALF, (2 * n + k + 1) * HALF)
            total = sum(p[at].astype(F32) for p in (p0, p1, p2))
            ref[here] = (total if k else total * DH**-0.5).astype(ref.dtype)


SMEM = pl.BlockSpec(memory_space=pltpu.SMEM)
VMEM = pl.BlockSpec(memory_space=pltpu.VMEM)
PARAMS = pltpu.CompilerParams(vmem_limit_bytes=48 * 1024 * 1024)
SDS = jax.ShapeDtypeStruct


def cost(us, size):
    return pl.CostEstimate(flops=us * 10**9, bytes_accessed=size, transcendentals=0)


def call(kernel, name, us, n_in, outs, scratch=(), smem=True):
    return pl.pallas_call(
        kernel,
        in_specs=[SMEM] * smem + [VMEM] * n_in,
        out_specs=[VMEM] * len(outs),
        out_shape=outs,
        scratch_shapes=list(scratch),
        compiler_params=PARAMS,
        cost_estimate=cost(us, 1 << 20),
        name=name,
    )


KEYS_S = pltpu.VMEM(((NB + PAD) * CH, DH), BF)
TURN_S = pltpu.VMEM((DH, (NB + PAD) * CH), BF)
GRAD_S = pltpu.VMEM(((NB + PAD) * CH, DH), F32)
ACC_S = pltpu.VMEM((DH, L), F32)
LINE_S = pltpu.VMEM((1, L), F32)


def run_forward(meta, keys, rows):
    return call(
        forward_kernel,
        "forward",
        12,
        9,
        [SDS((4, DH, HH * ROWS), BF), SDS((4, 3, HH * ROWS), F32)],
        [KEYS_S, TURN_S, ACC_S, LINE_S, LINE_S],
    )(meta, *keys, rows)


def run_backward(meta, keys, rows, ot, stats):
    *back, mine, theirs = call(
        backward_kernel,
        "backward",
        25,
        14,
        [SDS((2 * ROWS, HH * DH), BF)] * 3
        + [SDS((ROWS, HH * DH), BF)] * 2
        + [SDS((4, 4, CH, 2 * DH), BF)] * 2,
        [KEYS_S, KEYS_S, TURN_S, GRAD_S, GRAD_S, ACC_S]
        + [pltpu.VMEM((4, 2 * ROWS, HH * DH), BF)],
    )(meta, *keys, rows, ot, *stats)
    return back, mine, theirs


def shift(value, axis, by):
    return lax.ppermute(value, axis, [(i, (i + by) % 4) for i in range(4)])


def swap(value):
    return lax.ppermute(value, "core", [(0, 1), (1, 0)])


def gathered(value, axis):
    return [value] + [shift(value, axis, by) for by in SLOT[1:]]


def ring(value, axis):
    half = value.shape[0] // 2
    one, two = shift(value, axis, 1), shift(value, axis, 3)
    return [value, one, two, shift(one[:half], axis, 1), shift(two[half:], axis, 3)]


def sent_back(slots, axis):
    return [slots[0]] + [shift(slots[s], axis, 4 - SLOT[s]) for s in (1, 2, 3)]


def local(queries, keys, values, doc_ids, out_grad):
    meta = jnp.stack([lax.axis_index(a) for a in ("x", "y", "core", "z")]).astype(jnp.int32)
    packed = SDS((CH + 16, 2 * DH), BF)
    chunks = call(pack_kernel, "pack", 1, 3, [packed] * 4)(
        meta, keys, values, doc_ids.reshape(ROWS // DH, DH)
    )
    column = jnp.concatenate([chunks[0]] + [shift(chunks[s], "x", SLOT[s]) for s in (1, 2, 3)])
    near = gathered(column, "y")
    keys_all = near + [swap(n) for n in near]
    both = call(pair_kernel, "pair", 1, 2, [SDS((2 * ROWS, HH * DH), BF)], smem=False)
    stack = call(stack_kernel, "stack", 1, 5, [SDS((4, 2 * ROWS, HH * DH), BF)], smem=False)
    rows = stack(*ring(both(queries, out_grad)[0], "x"))[0]
    ot, st = run_forward(meta, keys_all, rows)
    stats = gathered(st, "x")
    (e0, e1, e2, e3a, e3b), mine, theirs = run_backward(meta, keys_all, rows, ot, stats)
    column = SDS((4, CH, 2 * DH), BF)
    chunk = SDS((CH, 2 * DH), BF)
    terms = call(join_kernel, "join", 1, 2, [column] * 4, smem=False)(mine, swap(theirs))
    parts = call(split_kernel, "split", 1, 4, [chunk] * 4)(meta, *sent_back(terms, "y"))
    parts = [parts[0]] + [shift(parts[k], "z", SLOT[k]) for k in (1, 2, 3)]
    one = call(sum_kernel, "sum", 1, 4, [chunk], smem=False)(*parts)[0]
    home = [(4 * a + z, (a - SLOT[z]) % 4 * 4 + z) for a in range(4) for z in range(4)]
    one = lax.ppermute(one, ("x", "z"), home)
    k_grad, v_grad = call(place_kernel, "place", 1, 4, [SDS((ROWS, DH), F32)] * 2)(
        meta, *gathered(one, "z")
    )
    relay = call(relay_kernel, "relay", 1, 4, [SDS((2 * ROWS, HH * DH), BF)] * 2, smem=False)
    e1, e2 = relay(e1, e2, shift(e3a, "x", 3), shift(e3b, "x", 1))
    finish = call(
        finish_kernel,
        "finish",
        1,
        3,
        [SDS((ROWS, HH * DH), BF), SDS((ROWS, HH * DH), F32)],
        smem=False,
    )
    attn_out, q_grad = finish(e0, shift(e1, "x", 3), shift(e2, "x", 1))
    return attn_out, q_grad, k_grad, v_grad


def solution(mesh):
    fine = Mesh(mesh.devices.reshape(4, 4, 2, 4), ("x", "y", "core", "z"))
    ctx = ("x", "y", "core")
    return jax.shard_map(
        local,
        mesh=fine,
        in_specs=(P(ctx, "z"), P(ctx, None), P(ctx, None), P(ctx), P(ctx, "z")),
        out_specs=(P(ctx, "z"), P(ctx, "z"), P(ctx, None), P(ctx, None)),
        check_vma=False,
    )
```

```python
import functools
import math

import jax
import jax.numpy as jnp
from jax import lax
from jax.experimental import pallas as pl
from jax.experimental.pallas import tpu as pltpu
from jax.sharding import Mesh, PartitionSpec as P

BF = jnp.bfloat16
F32 = jnp.float32
DH = 128
ROWS = 512
CH = 128
NB = 32
HH = 2
RG = 512
NG = ROWS // RG
HALF = ROWS // 2
L = HH * RG
TILE = 4
PAD = 4
SLOT = (0, 1, 3, 2)
LOW = -1e30
COEF = DH**-0.5 * math.log2(math.e)


def pieces_of(refs):
    for far in (0, 1):
        for t in range(4):
            for s in range(4):
                yield refs[4 * far + t], s * (CH + 16), s, t, far


def chunk_at(meta, s, t, far):
    x, y, core = meta[0], meta[1], meta[2]
    xb, yb = (x - SLOT[s] + 4) % 4, (y - SLOT[t] + 4) % 4
    par = 1 - core if far else core
    return pl.multiple_of((2 * (4 * xb + yb) + par) * CH, CH)


def load_keys(refs, meta, k_s, v_s, kt_s, vt_s):
    for ref, first, s, t, far in pieces_of(refs):
        at = chunk_at(meta, s, t, far)
        kc = ref[first : first + CH, :DH]
        vc = ref[first : first + CH, DH:]
        k_s[pl.ds(at, CH), :] = kc
        if v_s is not None:
            v_s[pl.ds(at, CH), :] = vc
        if kt_s is not None:
            kt_s[:, pl.ds(at, CH)] = kc.T
        if vt_s is not None:
            vt_s[:, pl.ds(at, CH)] = vc.T
    tail = NB * CH
    k_s[tail:, :] = jnp.zeros((PAD * CH, DH), BF)
    if v_s is not None:
        v_s[tail:, :] = jnp.zeros((PAD * CH, DH), BF)
    if kt_s is not None:
        kt_s[:, tail:] = jnp.zeros((DH, PAD * CH), BF)
    if vt_s is not None:
        vt_s[:, tail:] = jnp.zeros((DH, PAD * CH), BF)


def doc_starts(refs):
    docs = jnp.concatenate(
        [ref[first + CH : first + CH + 16, :] for ref, first, _, _, _ in pieces_of(refs)], axis=0
    ).astype(F32)
    return [jnp.sum(jnp.where(docs < d, 1.0, 0.0)).astype(jnp.int32) for d in (1, 2, 3)]


def start_of(pos, starts):
    begin = jnp.zeros_like(pos)
    for c in starts:
        begin = jnp.where(pos >= c, c, begin)
    return begin


def group_facts(meta, gi, starts):
    x, y, core = meta[0], meta[1], meta[2]
    slot = gi // NG
    r = gi % NG
    back = jnp.where(slot == 2, 3, jnp.where(slot == 3, 2, slot))
    xs = (x - back + 4) % 4
    row0 = (8 * xs + 2 * y + core) * ROWS + r * RG
    lane = lax.broadcasted_iota(jnp.int32, (1, L), 1)
    rpos = row0 + lane % RG
    ds = start_of(rpos, starts)
    ds_min = start_of(row0, starts)
    ds_max = start_of(row0 + RG - 1, starts)
    lo = (ds_min - CH * x + (ROWS - CH)) // ROWS
    end = (row0 + RG - 1 - CH * x + ROWS) // ROWS
    return slot, r, xs, row0, rpos, ds, ds_max, lo, jnp.maximum(0, end - lo)


def group_rows(ref, slot, which):
    at = which * HALF
    both = jnp.concatenate(
        [ref[slot, at : at + HALF, :], ref[slot, ROWS + at : ROWS + at + HALF, :]], axis=0
    )
    return both[:, :DH], both[:, DH:]


def keep_of(m0, x, rpos, ds, step):
    base = m0 * ROWS + x * CH
    i = lax.broadcasted_iota(jnp.int32, (step * CH, 1), 0)
    kpos = base + i + (ROWS - CH) * (i // CH)
    return (kpos <= rpos) & (kpos >= ds)


def is_whole(m0, x, row0, ds_max, step):
    first = m0 * ROWS + x * CH
    return (first + (step - 1) * ROWS + CH - 1 <= row0) & (first >= ds_max)


def over_tiles(lo, chunks, work):
    tiles = (chunks + 1) // TILE
    tail = chunks - tiles * TILE

    def whole(i, carry):
        work(lo + i * TILE, TILE)
        return carry

    lax.fori_loop(0, tiles, whole, 0)

    @pl.when(tail > 0)
    def rest():
        work(lo + tiles * TILE, TILE // 2)


def mm(a, b):
    return jnp.dot(a, b, preferred_element_type=F32)


def forward_kernel(
    meta, n0, n1, n2, n3, f0, f1, f2, f3, qg_s,
    ot_ref, st_ref, k_s, vt_s, acc_s, m_s, l_s,
):
    x = meta[0]
    refs = (n0, n1, n2, n3, f0, f1, f2, f3)
    load_keys(refs, meta, k_s, None, None, vt_s)
    starts = doc_starts(refs)

    def group(gi, carry):
        slot, r, xs, row0, rpos, ds, ds_max, lo, chunks = group_facts(meta, gi, starts)
        q0, q1 = group_rows(qg_s, slot, 0)
        qt = jnp.concatenate([q0.T, q1.T], axis=1)
        acc_s[...] = jnp.zeros_like(acc_s)
        m_s[...] = jnp.zeros_like(m_s)
        l_s[...] = jnp.zeros_like(l_s)

        def tile(m0, step):
            here = pl.ds(pl.multiple_of(m0 * CH, CH), step * CH)

            def work(masked):
                p = jnp.exp2(mm(k_s[here, :], qt) * COEF)
                if masked:
                    p = jnp.where(keep_of(m0, x, rpos, ds, step), p, 0.0)
                l_s[...] += jnp.sum(p, axis=0, keepdims=True)
                acc_s[...] += mm(vt_s[:, here], p.astype(BF))

            whole = is_whole(m0, x, row0, ds_max, step)
            pl.when(whole)(functools.partial(work, False))
            pl.when(jnp.logical_not(whole))(functools.partial(work, True))

        over_tiles(lo, chunks, tile)

        def careful_tile(m0, step):
            here = pl.ds(pl.multiple_of(m0 * CH, CH), step * CH)
            keep = keep_of(m0, x, rpos, ds, step)
            s = jnp.where(keep, mm(k_s[here, :], qt), LOW)
            m_old = m_s[...]
            m_new = jnp.maximum(m_old, jnp.max(s, axis=0, keepdims=True) * COEF)
            alpha = jnp.exp2(m_old - m_new)
            p = jnp.where(keep, jnp.exp2(s * COEF - m_new), 0.0)
            l_s[...] = l_s[...] * alpha + jnp.sum(p, axis=0, keepdims=True)
            m_s[...] = m_new
            acc_s[...] = acc_s[...] * alpha + mm(vt_s[:, here], p.astype(BF))

        block = (rpos - CH * x) >> 9
        last = jnp.minimum(rpos, block * ROWS + CH * x + CH - 1)
        some = (block >= 0) & (last >= ds)
        l = l_s[...]
        good = (jnp.min(jnp.where(some, l, 1.0)) >= 2.0**-60) & (jnp.max(l) <= 2.0**60)

        @pl.when(jnp.logical_not(good))
        def careful():
            acc_s[...] = jnp.zeros_like(acc_s)
            m_s[...] = jnp.full_like(m_s, LOW)
            l_s[...] = jnp.zeros_like(l_s)
            over_tiles(lo, chunks, careful_tile)

        g0, g1 = group_rows(qg_s, slot, 1)
        gt = jnp.concatenate([g0.T, g1.T], axis=1).astype(F32)
        acc = acc_s[...]
        l = l_s[...]
        lanes = pl.ds(pl.multiple_of(r * L, L), L)
        ot_ref[slot, :, lanes] = (acc / jnp.where(l > 0, l, 1.0)).astype(BF)
        st_ref[xs, 0:1, lanes] = m_s[...]
        st_ref[xs, 1:2, lanes] = l
        st_ref[xs, 2:3, lanes] = jnp.sum(acc * gt, axis=0, keepdims=True)
        return carry

    lax.fori_loop(0, 4 * NG, group, 0)


def merged(sts):
    top = functools.reduce(jnp.maximum, [st[0:1] for st in sts])
    scale = [jnp.exp2(st[0:1] - top) for st in sts]
    total = sum(st[1:2] * f for st, f in zip(sts, scale))
    delta = sum(st[2:3] * f for st, f in zip(sts, scale)) / total
    return top + jnp.log2(total), delta, sts[0][1:2] * scale[0] / total


def backward_kernel(
    meta, n0, n1, n2, n3, f0, f1, f2, f3, qg_s,
    ot_ref, s0, s1, s2, s3, e0, e1, e2, e3a, e3b, mine_ref, theirs_ref,
    k_s, v_s, kt_s, dk_s, dv_s, acc_s, back_s,
):
    x = meta[0]
    refs = (n0, n1, n2, n3, f0, f1, f2, f3)
    load_keys(refs, meta, k_s, v_s, kt_s, None)
    starts = doc_starts(refs)
    dk_s[...] = jnp.zeros_like(dk_s)
    dv_s[...] = jnp.zeros_like(dv_s)

    def group(gi, carry):
        slot, r, xs, row0, rpos, ds, ds_max, lo, chunks = group_facts(meta, gi, starts)
        q0, q1 = group_rows(qg_s, slot, 0)
        g0, g1 = group_rows(qg_s, slot, 1)
        qt = jnp.concatenate([q0.T, q1.T], axis=1)
        gt = jnp.concatenate([g0.T, g1.T], axis=1)
        qm = jnp.concatenate([q0, q1], axis=0)
        gm = jnp.concatenate([g0, g1], axis=0)
        lanes = pl.ds(pl.multiple_of(r * L, L), L)
        lse, delta, share = merged([st[xs, :, lanes] for st in (s0, s1, s2, s3)])
        acc_s[...] = jnp.zeros_like(acc_s)

        def tile(m0, step):
            here = pl.ds(pl.multiple_of(m0 * CH, CH), step * CH)

            def work(masked):
                s = mm(k_s[here, :], qt)
                p = jnp.exp2(s * COEF - lse)
                if masked:
                    p = jnp.where(keep_of(m0, x, rpos, ds, step), p, 0.0)
                dp = mm(v_s[here, :], gt)
                dsc = (p * (dp - delta)).astype(BF)
                dv_s[here, :] += mm(p.astype(BF), gm)
                dk_s[here, :] += mm(dsc, qm)
                acc_s[...] += mm(kt_s[:, here], dsc)

            whole = is_whole(m0, x, row0, ds_max, step)
            pl.when(whole)(functools.partial(work, False))
            pl.when(jnp.logical_not(whole))(functools.partial(work, True))

        over_tiles(lo, chunks, tile)
        acc = acc_s[...]
        out = ot_ref[slot, :, lanes].astype(F32) * share
        for h in range(HH):
            cols = slice(h * DH, (h + 1) * DH)
            for n in range(2):
                part = slice(h * RG + n * HALF, h * RG + (n + 1) * HALF)
                back_s[slot, (2 * n) * HALF : (2 * n + 1) * HALF, cols] = acc[:, part].T.astype(BF)
                back_s[slot, (2 * n + 1) * HALF : (2 * n + 2) * HALF, cols] = out[:, part].T.astype(BF)
        return carry

    lax.fori_loop(0, 4 * NG, group, 0)
    for slot, ref in enumerate((e0, e1, e2)):
        ref[...] = back_s[slot]
    e3a[...] = back_s[3, :ROWS]
    e3b[...] = back_s[3, ROWS:]
    for t in range(4):
        for s in range(4):
            for far, ref in ((0, mine_ref), (1, theirs_ref)):
                at = pl.ds(chunk_at(meta, s, t, far), CH)
                ref[t, s, :, :DH] = dk_s[at, :].astype(BF)
                ref[t, s, :, DH:] = dv_s[at, :].astype(BF)


def pack_kernel(meta, keys_ref, values_ref, docs_ref, *outs):
    rest = jnp.full((16 - ROWS // DH, DH), 3.0, F32)
    docs = jnp.concatenate([docs_ref[...].astype(F32), rest], axis=0)
    docs = jnp.concatenate([docs, jnp.full((16, DH), 3.0, F32)], axis=1).astype(BF)
    for s, ref in enumerate(outs):
        at = pl.ds(pl.multiple_of((meta[0] + SLOT[s]) % 4 * CH, CH), CH)
        ref[:CH, :DH] = keys_ref[at, :]
        ref[:CH, DH:] = values_ref[at, :]
        ref[CH:, :] = docs


def pair_kernel(q_ref, g_ref, after1, after2, after3, out_ref):
    for n in range(2):
        here = slice(n * HALF, (n + 1) * HALF)
        out_ref[2 * n * HALF : (2 * n + 1) * HALF] = q_ref[here]
        out_ref[(2 * n + 1) * HALF : (2 * n + 2) * HALF] = g_ref[here]


def stack_kernel(p0, p1, p2, p3a, p3b, out_ref):
    for s, ref in enumerate((p0, p1, p2)):
        out_ref[s] = ref[...]
    out_ref[3, :ROWS] = p3a[...]
    out_ref[3, ROWS:] = p3b[...]


def join_kernel(mine_ref, theirs_ref, *outs):
    for t, ref in enumerate(outs):
        ref[...] = (mine_ref[t].astype(F32) + theirs_ref[t].astype(F32)).astype(BF)


def sum_kernel(p0, p1, p2, p3, out_ref):
    out_ref[...] = sum(p[...].astype(F32) for p in (p0, p1, p2, p3)).astype(BF)


def split_kernel(meta, p0, p1, p2, p3, *outs):
    for k, ref in enumerate(outs):
        s = (meta[3] + k) % 4
        ref[...] = sum(p[s].astype(F32) for p in (p0, p1, p2, p3)).astype(BF)


def place_kernel(meta, p0, p1, p2, p3, dk_ref, dv_ref):
    for k, ref in enumerate((p0, p1, p2, p3)):
        s = (meta[3] - SLOT[k] + 4) % 4
        step = jnp.where(s == 2, 3, jnp.where(s == 3, 2, s))
        at = pl.ds(pl.multiple_of((meta[0] + step) % 4 * CH, CH), CH)
        dk_ref[at, :] = ref[:, :DH].astype(F32) * DH**-0.5
        dv_ref[at, :] = ref[:, DH:].astype(F32)


def relay_kernel(e1, e2, ra, rb, o1, o2):
    o1[:ROWS] = (e1[:ROWS].astype(F32) + ra[...].astype(F32)).astype(BF)
    o1[ROWS:] = e1[ROWS:]
    o2[:ROWS] = e2[:ROWS]
    o2[ROWS:] = (e2[ROWS:].astype(F32) + rb[...].astype(F32)).astype(BF)


def finish_kernel(p0, p1, p2, out_ref, dq_ref):
    for n in range(2):
        here = slice(n * HALF, (n + 1) * HALF)
        for k, ref in ((0, dq_ref), (1, out_ref)):
            at = slice((2 * n + k) * HALF, (2 * n + k + 1) * HALF)
            total = sum(p[at].astype(F32) for p in (p0, p1, p2))
            ref[here] = (total if k else total * DH**-0.5).astype(ref.dtype)


SMEM = pl.BlockSpec(memory_space=pltpu.SMEM)
VMEM = pl.BlockSpec(memory_space=pltpu.VMEM)
PARAMS = pltpu.CompilerParams(vmem_limit_bytes=32 * 1024 * 1024)
SDS = jax.ShapeDtypeStruct


def cost(us, size):
    return pl.CostEstimate(flops=us * 10**9, bytes_accessed=size, transcendentals=0)


def call(kernel, name, us, n_in, outs, scratch=(), smem=True):
    return pl.pallas_call(
        kernel,
        in_specs=[SMEM] * smem + [VMEM] * n_in,
        out_specs=[VMEM] * len(outs),
        out_shape=outs,
        scratch_shapes=list(scratch),
        compiler_params=PARAMS,
        cost_estimate=cost(us, 1 << 20),
        name=name,
    )


KEYS_S = pltpu.VMEM(((NB + PAD) * CH, DH), BF)
TURN_S = pltpu.VMEM((DH, (NB + PAD) * CH), BF)
GRAD_S = pltpu.VMEM(((NB + PAD) * CH, DH), F32)
ACC_S = pltpu.VMEM((DH, L), F32)
LINE_S = pltpu.VMEM((1, L), F32)


def run_forward(meta, keys, rows):
    return call(
        forward_kernel,
        "forward",
        12,
        9,
        [SDS((4, DH, HH * ROWS), BF), SDS((4, 3, HH * ROWS), F32)],
        [KEYS_S, TURN_S, ACC_S, LINE_S, LINE_S],
    )(meta, *keys, rows)


def run_backward(meta, keys, rows, ot, stats):
    *back, mine, theirs = call(
        backward_kernel,
        "backward",
        25,
        14,
        [SDS((2 * ROWS, HH * DH), BF)] * 3
        + [SDS((ROWS, HH * DH), BF)] * 2
        + [SDS((4, 4, CH, 2 * DH), BF)] * 2,
        [KEYS_S, KEYS_S, TURN_S, GRAD_S, GRAD_S, ACC_S]
        + [pltpu.VMEM((4, 2 * ROWS, HH * DH), BF)],
    )(meta, *keys, rows, ot, *stats)
    return back, mine, theirs


def shift(value, axis, by):
    return lax.ppermute(value, axis, [(i, (i + by) % 4) for i in range(4)])


def swap(value):
    return lax.ppermute(value, "core", [(0, 1), (1, 0)])


def gathered(value, axis):
    return [value] + [shift(value, axis, by) for by in SLOT[1:]]


def ring(value, axis):
    half = value.shape[0] // 2
    one, two = shift(value, axis, 1), shift(value, axis, 3)
    return [value, one, two, shift(one[:half], axis, 1), shift(two[half:], axis, 3)]


def sent_back(slots, axis):
    return [slots[0]] + [shift(slots[s], axis, 4 - SLOT[s]) for s in (1, 2, 3)]


def local(queries, keys, values, doc_ids, out_grad):
    meta = jnp.stack([lax.axis_index(a) for a in ("x", "y", "core", "z")]).astype(jnp.int32)
    packed = SDS((CH + 16, 2 * DH), BF)
    chunks = call(pack_kernel, "pack", 1, 3, [packed] * 4)(
        meta, keys, values, doc_ids.reshape(ROWS // DH, DH)
    )
    came = [shift(chunks[s], "x", SLOT[s]) for s in (1, 2, 3)]
    column = jnp.concatenate([chunks[0]] + came)
    near = gathered(column, "y")
    keys_all = near + [swap(n) for n in near]
    both = call(pair_kernel, "pair", 1, 5, [SDS((2 * ROWS, HH * DH), BF)], smem=False)
    stack = call(stack_kernel, "stack", 1, 5, [SDS((4, 2 * ROWS, HH * DH), BF)], smem=False)
    rows = stack(*ring(both(queries, out_grad, *came)[0], "x"))[0]
    ot, st = run_forward(meta, keys_all, rows)
    stats = gathered(st, "x")
    (e0, e1, e2, e3a, e3b), mine, theirs = run_backward(meta, keys_all, rows, ot, stats)
    column = SDS((4, CH, 2 * DH), BF)
    chunk = SDS((CH, 2 * DH), BF)
    terms = call(join_kernel, "join", 1, 2, [column] * 4, smem=False)(mine, swap(theirs))
    parts = call(split_kernel, "split", 1, 4, [chunk] * 4)(meta, *sent_back(terms, "y"))
    parts = [
        lax.ppermute(
            parts[k],
            ("x", "z"),
            [
                (4 * a + z, (a - SLOT[(z + k) % 4]) % 4 * 4 + (z + k) % 4)
                for a in range(4)
                for z in range(4)
            ],
        )
        for k in range(4)
    ]
    one = call(sum_kernel, "sum", 1, 4, [chunk], smem=False)(*parts)[0]
    k_grad, v_grad = call(place_kernel, "place", 1, 4, [SDS((ROWS, DH), F32)] * 2)(
        meta, *gathered(one, "z")
    )
    relay = call(relay_kernel, "relay", 1, 4, [SDS((2 * ROWS, HH * DH), BF)] * 2, smem=False)
    e1, e2 = relay(e1, e2, shift(e3a, "x", 3), shift(e3b, "x", 1))
    finish = call(
        finish_kernel,
        "finish",
        1,
        3,
        [SDS((ROWS, HH * DH), BF), SDS((ROWS, HH * DH), F32)],
        smem=False,
    )
    attn_out, q_grad = finish(e0, shift(e1, "x", 3), shift(e2, "x", 1))
    return attn_out, q_grad, k_grad, v_grad


def solution(mesh):
    fine = Mesh(mesh.devices.reshape(4, 4, 2, 4), ("x", "y", "core", "z"))
    ctx = ("x", "y", "core")
    return jax.shard_map(
        local,
        mesh=fine,
        in_specs=(P(ctx, "z"), P(ctx, None), P(ctx, None), P(ctx), P(ctx, "z")),
        out_specs=(P(ctx, "z"), P(ctx, "z"), P(ctx, None), P(ctx, None)),
        check_vma=False,
    )
```

```python
import functools
import math

import jax
import jax.numpy as jnp
from jax import lax
from jax.experimental import pallas as pl
from jax.experimental.pallas import tpu as pltpu
from jax.sharding import Mesh, PartitionSpec as P

BF = jnp.bfloat16
F32 = jnp.float32
DH = 128
ROWS = 512
CH = 128
NB = 32
HH = 2
RG = 512
NG = ROWS // RG
HALF = ROWS // 2
L = HH * RG
TILE = 4
PAD = 4
SLOT = (0, 1, 3, 2)
LOW = -1e30
COEF = DH**-0.5 * math.log2(math.e)


def pieces_of(refs):
    for far in (0, 1):
        for t in range(4):
            for s in range(4):
                yield refs[4 * far + t], s * (CH + 16), s, t, far


def chunk_at(meta, s, yb, far):
    x, core = meta[0], meta[2]
    xb = (x - SLOT[s] + 4) % 4
    par = 1 - core if far else core
    return pl.multiple_of((2 * (4 * xb + yb) + par) * CH, CH)


def load_keys(refs, meta, k_s, v_s, kt_s, vt_s):
    for ref, first, s, t, far in pieces_of(refs):
        at = chunk_at(meta, s, (meta[1] - SLOT[t] + 4) % 4, far)
        kc = ref[first : first + CH, :DH]
        vc = ref[first : first + CH, DH:]
        k_s[pl.ds(at, CH), :] = kc
        if v_s is not None:
            v_s[pl.ds(at, CH), :] = vc
        if kt_s is not None:
            kt_s[:, pl.ds(at, CH)] = kc.T
        if vt_s is not None:
            vt_s[:, pl.ds(at, CH)] = vc.T
    tail = NB * CH
    k_s[tail:, :] = jnp.zeros((PAD * CH, DH), BF)
    if v_s is not None:
        v_s[tail:, :] = jnp.zeros((PAD * CH, DH), BF)
    if kt_s is not None:
        kt_s[:, tail:] = jnp.zeros((DH, PAD * CH), BF)
    if vt_s is not None:
        vt_s[:, tail:] = jnp.zeros((DH, PAD * CH), BF)


def doc_starts(refs):
    docs = jnp.concatenate(
        [ref[first + CH : first + CH + 16, :] for ref, first, _, _, _ in pieces_of(refs)], axis=0
    ).astype(F32)
    return [jnp.sum(jnp.where(docs < d, 1.0, 0.0)).astype(jnp.int32) for d in (1, 2, 3)]


def start_of(pos, starts):
    begin = jnp.zeros_like(pos)
    for c in starts:
        begin = jnp.where(pos >= c, c, begin)
    return begin


def group_facts(meta, gi, starts):
    x, y, core = meta[0], meta[1], meta[2]
    slot = gi // NG
    r = gi % NG
    back = jnp.where(slot == 2, 3, jnp.where(slot == 3, 2, slot))
    xs = (x - back + 4) % 4
    row0 = (8 * xs + 2 * y + core) * ROWS + r * RG
    lane = lax.broadcasted_iota(jnp.int32, (1, L), 1)
    rpos = row0 + lane % RG
    ds = start_of(rpos, starts)
    ds_min = start_of(row0, starts)
    ds_max = start_of(row0 + RG - 1, starts)
    lo = (ds_min - CH * x + (ROWS - CH)) // ROWS
    end = (row0 + RG - 1 - CH * x + ROWS) // ROWS
    return slot, r, xs, row0, rpos, ds, ds_max, lo, jnp.maximum(0, end - lo)


def group_rows(ref, slot, which):
    at = which * HALF
    both = jnp.concatenate(
        [ref[slot, at : at + HALF, :], ref[slot, ROWS + at : ROWS + at + HALF, :]], axis=0
    )
    return both[:, :DH], both[:, DH:]


def keep_of(m0, x, rpos, ds, step, causal=True, inside=True):
    base = m0 * ROWS + x * CH
    i = lax.broadcasted_iota(jnp.int32, (step * CH, 1), 0)
    kpos = base + i + (ROWS - CH) * (i // CH)
    if causal and inside:
        return (kpos <= rpos) & (kpos >= ds)
    return kpos <= rpos if causal else kpos >= ds


def by_mask(m0, x, row0, ds_max, step, work):
    first = m0 * ROWS + x * CH
    causal = first + (step - 1) * ROWS + CH - 1 > row0
    inside = first < ds_max
    for c in (False, True):
        for d in (False, True):
            pl.when((causal == c) & (inside == d))(functools.partial(work, c, d))


def over_tiles(lo, chunks, work):
    tiles = (chunks + 1) // TILE
    tail = chunks - tiles * TILE

    def whole(i, carry):
        work(lo + i * TILE, TILE)
        return carry

    lax.fori_loop(0, tiles, whole, 0)

    @pl.when(tail > 0)
    def rest():
        work(lo + tiles * TILE, TILE // 2)


def mm(a, b):
    return jnp.dot(a, b, preferred_element_type=F32)


def forward_kernel(
    meta, n0, n1, n2, n3, f0, f1, f2, f3, qg_s,
    ot_ref, st_ref, k_s, vt_s, acc_s, m_s, l_s,
):
    x = meta[0]
    refs = (n0, n1, n2, n3, f0, f1, f2, f3)
    load_keys(refs, meta, k_s, None, None, vt_s)
    starts = doc_starts(refs)

    def group(gi, carry):
        slot, r, xs, row0, rpos, ds, ds_max, lo, chunks = group_facts(meta, gi, starts)
        q0, q1 = group_rows(qg_s, slot, 0)
        qt = jnp.concatenate([q0.T, q1.T], axis=1)
        acc_s[...] = jnp.zeros_like(acc_s)
        m_s[...] = jnp.zeros_like(m_s)
        l_s[...] = jnp.zeros_like(l_s)

        def tile(m0, step):
            here = pl.ds(pl.multiple_of(m0 * CH, CH), step * CH)

            def work(causal, inside):
                p = jnp.exp2(mm(k_s[here, :], qt) * COEF)
                if causal or inside:
                    p = jnp.where(keep_of(m0, x, rpos, ds, step, causal, inside), p, 0.0)
                l_s[...] += jnp.sum(p, axis=0, keepdims=True)
                acc_s[...] += mm(vt_s[:, here], p.astype(BF))

            by_mask(m0, x, row0, ds_max, step, work)

        over_tiles(lo, chunks, tile)

        def careful_tile(i, carry):
            step = TILE // 2
            m0 = lo + i * step
            here = pl.ds(pl.multiple_of(m0 * CH, CH), step * CH)
            keep = keep_of(m0, x, rpos, ds, step)
            s = jnp.where(keep, mm(k_s[here, :], qt), LOW)
            m_old = m_s[...]
            m_new = jnp.maximum(m_old, jnp.max(s, axis=0, keepdims=True) * COEF)
            alpha = jnp.exp2(m_old - m_new)
            p = jnp.where(keep, jnp.exp2(s * COEF - m_new), 0.0)
            l_s[...] = l_s[...] * alpha + jnp.sum(p, axis=0, keepdims=True)
            m_s[...] = m_new
            acc_s[...] = acc_s[...] * alpha + mm(vt_s[:, here], p.astype(BF))
            return carry

        block = (rpos - CH * x) >> 9
        last = jnp.minimum(rpos, block * ROWS + CH * x + CH - 1)
        some = (block >= 0) & (last >= ds)
        l = l_s[...]
        good = (jnp.min(jnp.where(some, l, 1.0)) >= 2.0**-60) & (jnp.max(l) <= 2.0**60)

        @pl.when(jnp.logical_not(good))
        def careful():
            acc_s[...] = jnp.zeros_like(acc_s)
            m_s[...] = jnp.full_like(m_s, LOW)
            l_s[...] = jnp.zeros_like(l_s)
            lax.fori_loop(0, (chunks + TILE // 2 - 1) // (TILE // 2), careful_tile, 0)

        g0, g1 = group_rows(qg_s, slot, 1)
        gt = jnp.concatenate([g0.T, g1.T], axis=1).astype(F32)
        acc = acc_s[...]
        l = l_s[...]
        lanes = pl.ds(pl.multiple_of(r * L, L), L)
        ot_ref[slot, :, lanes] = (acc / jnp.where(l > 0, l, 1.0)).astype(BF)
        st_ref[xs, 0:1, lanes] = m_s[...]
        st_ref[xs, 1:2, lanes] = l
        st_ref[xs, 2:3, lanes] = jnp.sum(acc * gt, axis=0, keepdims=True)
        return carry

    lax.fori_loop(0, 4 * NG, group, 0)


def merged(sts):
    top = functools.reduce(jnp.maximum, [st[0:1] for st in sts])
    scale = [jnp.exp2(st[0:1] - top) for st in sts]
    total = sum(st[1:2] * f for st, f in zip(sts, scale))
    delta = sum(st[2:3] * f for st, f in zip(sts, scale)) / total
    return top + jnp.log2(total), delta, sts[0][1:2] * scale[0] / total


def backward_kernel(
    meta, n0, n1, n2, n3, f0, f1, f2, f3, qg_s,
    ot_ref, s0, s1, s2, s3, e0, e1, e2, e3a, e3b, mine_ref, theirs_ref,
    k_s, v_s, kt_s, dk_s, dv_s, acc_s, back_s,
):
    x = meta[0]
    refs = (n0, n1, n2, n3, f0, f1, f2, f3)
    load_keys(refs, meta, k_s, v_s, kt_s, None)
    starts = doc_starts(refs)
    dk_s[...] = jnp.zeros_like(dk_s)
    dv_s[...] = jnp.zeros_like(dv_s)

    def group(gi, carry):
        slot, r, xs, row0, rpos, ds, ds_max, lo, chunks = group_facts(meta, gi, starts)
        q0, q1 = group_rows(qg_s, slot, 0)
        g0, g1 = group_rows(qg_s, slot, 1)
        qt = jnp.concatenate([q0.T, q1.T], axis=1)
        gt = jnp.concatenate([g0.T, g1.T], axis=1)
        qm = jnp.concatenate([q0, q1], axis=0)
        gm = jnp.concatenate([g0, g1], axis=0)
        lanes = pl.ds(pl.multiple_of(r * L, L), L)
        lse, delta, share = merged([st[xs, :, lanes] for st in (s0, s1, s2, s3)])
        acc_s[...] = jnp.zeros_like(acc_s)

        def tile(m0, step):
            here = pl.ds(pl.multiple_of(m0 * CH, CH), step * CH)

            def work(causal, inside):
                s = mm(k_s[here, :], qt)
                p = jnp.exp2(s * COEF - lse)
                if causal or inside:
                    p = jnp.where(keep_of(m0, x, rpos, ds, step, causal, inside), p, 0.0)
                dp = mm(v_s[here, :], gt)
                dsc = (p * (dp - delta)).astype(BF)
                dv_s[here, :] += mm(p.astype(BF), gm)
                dk_s[here, :] += mm(dsc, qm)
                acc_s[...] += mm(kt_s[:, here], dsc)

            by_mask(m0, x, row0, ds_max, step, work)

        over_tiles(lo, chunks, tile)
        acc = acc_s[...]
        out = ot_ref[slot, :, lanes].astype(F32) * share
        for h in range(HH):
            cols = slice(h * DH, (h + 1) * DH)
            for n in range(2):
                part = slice(h * RG + n * HALF, h * RG + (n + 1) * HALF)
                back_s[slot, (2 * n) * HALF : (2 * n + 1) * HALF, cols] = acc[:, part].T.astype(BF)
                back_s[slot, (2 * n + 1) * HALF : (2 * n + 2) * HALF, cols] = out[:, part].T.astype(BF)
        return carry

    lax.fori_loop(0, 4 * NG, group, 0)
    for slot, ref in enumerate((e0, e1, e2)):
        ref[...] = back_s[slot]
    e3a[...] = back_s[3, :ROWS]
    e3b[...] = back_s[3, ROWS:]
    for t in range(4):
        yb = (meta[1] - SLOT[t] + 4) % 4
        for s in range(4):
            for far, ref in ((0, mine_ref), (1, theirs_ref)):
                at = pl.ds(chunk_at(meta, s, yb, far), CH)
                ref[t, s, :, :DH] = dk_s[at, :].astype(BF)
                ref[t, s, :, DH:] = dv_s[at, :].astype(BF)


def pack_kernel(meta, keys_ref, values_ref, docs_ref, *outs):
    rest = jnp.full((16 - ROWS // DH, DH), 3.0, F32)
    docs = jnp.concatenate([docs_ref[...].astype(F32), rest], axis=0)
    docs = jnp.concatenate([docs, jnp.full((16, DH), 3.0, F32)], axis=1).astype(BF)
    for s, ref in enumerate(outs):
        at = pl.ds(pl.multiple_of((meta[0] + SLOT[s]) % 4 * CH, CH), CH)
        ref[:CH, :DH] = keys_ref[at, :]
        ref[:CH, DH:] = values_ref[at, :]
        ref[CH:, :] = docs


def pair_kernel(q_ref, g_ref, after1, after2, after3, out_ref):
    for n in range(2):
        here = slice(n * HALF, (n + 1) * HALF)
        out_ref[2 * n * HALF : (2 * n + 1) * HALF] = q_ref[here]
        out_ref[(2 * n + 1) * HALF : (2 * n + 2) * HALF] = g_ref[here]


def stack_kernel(p0, p1, p2, p3a, p3b, out_ref):
    for s, ref in enumerate((p0, p1, p2)):
        out_ref[s] = ref[...]
    out_ref[3, :ROWS] = p3a[...]
    out_ref[3, ROWS:] = p3b[...]


def join_kernel(mine_ref, theirs_ref, *outs):
    for t, ref in enumerate(outs):
        ref[...] = (mine_ref[t].astype(F32) + theirs_ref[t].astype(F32)).astype(BF)


def split_kernel(meta, p0, p1, p2, p3, *outs):
    for k, ref in enumerate(outs):
        s = (meta[3] + SLOT[k]) % 4
        ref[...] = sum(p[s].astype(F32) for p in (p0, p1, p2, p3)).astype(BF)


def sum_kernel(p0, p1, p2, p3, out_ref):
    out_ref[...] = sum(p[...].astype(F32) for p in (p0, p1, p2, p3)).astype(BF)


def place_kernel(meta, p0, p1, p2, p3, dk_ref, dv_ref):
    for k, ref in enumerate((p0, p1, p2, p3)):
        s = (meta[3] - k + 4) % 4
        step = jnp.where(s == 2, 3, jnp.where(s == 3, 2, s))
        at = pl.ds(pl.multiple_of((meta[0] + step) % 4 * CH, CH), CH)
        dk_ref[at, :] = ref[:, :DH].astype(F32) * DH**-0.5
        dv_ref[at, :] = ref[:, DH:].astype(F32)


def relay_kernel(e1, e2, ra, rb, after, o1, o2):
    o1[:ROWS] = (e1[:ROWS].astype(F32) + ra[...].astype(F32)).astype(BF)
    o1[ROWS:] = e1[ROWS:]
    o2[:ROWS] = e2[:ROWS]
    o2[ROWS:] = (e2[ROWS:].astype(F32) + rb[...].astype(F32)).astype(BF)


def finish_kernel(p0, p1, p2, out_ref, dq_ref):
    for n in range(2):
        here = slice(n * HALF, (n + 1) * HALF)
        for k, ref in ((0, dq_ref), (1, out_ref)):
            at = slice((2 * n + k) * HALF, (2 * n + k + 1) * HALF)
            total = sum(p[at].astype(F32) for p in (p0, p1, p2))
            ref[here] = (total if k else total * DH**-0.5).astype(ref.dtype)


SMEM = pl.BlockSpec(memory_space=pltpu.SMEM)
VMEM = pl.BlockSpec(memory_space=pltpu.VMEM)
PARAMS = pltpu.CompilerParams(vmem_limit_bytes=32 * 1024 * 1024)
SDS = jax.ShapeDtypeStruct


def cost(us, size):
    return pl.CostEstimate(flops=us * 10**9, bytes_accessed=size, transcendentals=0)


def call(kernel, name, us, n_in, outs, scratch=(), smem=True):
    return pl.pallas_call(
        kernel,
        in_specs=[SMEM] * smem + [VMEM] * n_in,
        out_specs=[VMEM] * len(outs),
        out_shape=outs,
        scratch_shapes=list(scratch),
        compiler_params=PARAMS,
        cost_estimate=cost(us, 1 << 20),
        name=name,
    )


KEYS_S = pltpu.VMEM(((NB + PAD) * CH, DH), BF)
TURN_S = pltpu.VMEM((DH, (NB + PAD) * CH), BF)
GRAD_S = pltpu.VMEM(((NB + PAD) * CH, DH), F32)
ACC_S = pltpu.VMEM((DH, L), F32)
LINE_S = pltpu.VMEM((1, L), F32)


def run_forward(meta, keys, rows):
    return call(
        forward_kernel,
        "forward",
        12,
        9,
        [SDS((4, DH, HH * ROWS), BF), SDS((4, 3, HH * ROWS), F32)],
        [KEYS_S, TURN_S, ACC_S, LINE_S, LINE_S],
    )(meta, *keys, rows)


def run_backward(meta, keys, rows, ot, stats):
    *back, mine, theirs = call(
        backward_kernel,
        "backward",
        25,
        14,
        [SDS((2 * ROWS, HH * DH), BF)] * 3
        + [SDS((ROWS, HH * DH), BF)] * 2
        + [SDS((4, 4, CH, 2 * DH), BF)] * 2,
        [KEYS_S, KEYS_S, TURN_S, GRAD_S, GRAD_S, ACC_S]
        + [pltpu.VMEM((4, 2 * ROWS, HH * DH), BF)],
    )(meta, *keys, rows, ot, *stats)
    return back, mine, theirs


def shift(value, axis, by):
    return lax.ppermute(value, axis, [(i, (i + by) % 4) for i in range(4)])


def swap(value):
    return lax.ppermute(value, "core", [(0, 1), (1, 0)])


def gathered(value, axis):
    return [value] + [shift(value, axis, by) for by in SLOT[1:]]


def ring(value, axis):
    half = value.shape[0] // 2
    one, two = shift(value, axis, 1), shift(value, axis, 3)
    return [value, one, two, shift(one[:half], axis, 1), shift(two[half:], axis, 3)]


def sent_back(slots, axis):
    return [slots[0]] + [shift(slots[s], axis, 4 - SLOT[s]) for s in (1, 2, 3)]


def local(queries, keys, values, doc_ids, out_grad):
    meta = jnp.stack([lax.axis_index(a) for a in ("x", "y", "core", "z")]).astype(jnp.int32)
    packed = SDS((CH + 16, 2 * DH), BF)
    chunks = call(pack_kernel, "pack", 1, 3, [packed] * 4)(
        meta, keys, values, doc_ids.reshape(ROWS // DH, DH)
    )
    came = [shift(chunks[s], "x", SLOT[s]) for s in (1, 2, 3)]
    column = jnp.concatenate([chunks[0]] + came)
    near = gathered(column, "y")
    keys_all = near + [swap(n) for n in near]
    both = call(pair_kernel, "pair", 1, 5, [SDS((2 * ROWS, HH * DH), BF)], smem=False)
    stack = call(stack_kernel, "stack", 1, 5, [SDS((4, 2 * ROWS, HH * DH), BF)], smem=False)
    rows = stack(*ring(both(queries, out_grad, *came)[0], "x"))[0]
    ot, st = run_forward(meta, keys_all, rows)
    stats = gathered(st, "x")
    (e0, e1, e2, e3a, e3b), mine, theirs = run_backward(meta, keys_all, rows, ot, stats)
    column = SDS((4, CH, 2 * DH), BF)
    chunk = SDS((CH, 2 * DH), BF)
    terms = call(join_kernel, "join", 1, 2, [column] * 4, smem=False)(mine, swap(theirs))
    parts = call(split_kernel, "split", 1, 4, [chunk] * 4)(meta, *sent_back(terms, "y"))
    parts = [parts[0]] + [shift(parts[k], "z", SLOT[k]) for k in (1, 2, 3)]
    total = call(sum_kernel, "sum", 1, 4, [chunk], smem=False)(*parts)[0]
    every = [
        lax.ppermute(
            total,
            ("x", "z"),
            [
                (4 * a + z, (a - SLOT[z]) % 4 * 4 + (z + k) % 4)
                for a in range(4)
                for z in range(4)
            ],
        )
        for k in range(4)
    ]
    k_grad, v_grad = call(place_kernel, "place", 1, 4, [SDS((ROWS, DH), F32)] * 2)(meta, *every)
    relay = call(relay_kernel, "relay", 1, 5, [SDS((2 * ROWS, HH * DH), BF)] * 2, smem=False)
    e1, e2 = relay(e1, e2, shift(e3a, "x", 3), shift(e3b, "x", 1), terms[0])
    finish = call(
        finish_kernel,
        "finish",
        1,
        3,
        [SDS((ROWS, HH * DH), BF), SDS((ROWS, HH * DH), F32)],
        smem=False,
    )
    attn_out, q_grad = finish(e0, shift(e1, "x", 3), shift(e2, "x", 1))
    return attn_out, q_grad, k_grad, v_grad


def solution(mesh):
    fine = Mesh(mesh.devices.reshape(4, 4, 2, 4), ("x", "y", "core", "z"))
    ctx = ("x", "y", "core")
    return jax.shard_map(
        local,
        mesh=fine,
        in_specs=(P(ctx, "z"), P(ctx, None), P(ctx, None), P(ctx), P(ctx, "z")),
        out_specs=(P(ctx, "z"), P(ctx, "z"), P(ctx, None), P(ctx, None)),
        check_vma=False,
    )
```

```python
import functools
import math

import jax
import jax.numpy as jnp
from jax import lax
from jax.experimental import pallas as pl
from jax.experimental.pallas import tpu as pltpu
from jax.sharding import Mesh, PartitionSpec as P

BF = jnp.bfloat16
F32 = jnp.float32
DH = 128
ROWS = 512
CH = 128
NB = 32
HH = 2
RG = 256
NG = ROWS // RG
HALF = ROWS // 2
L = HH * RG
TILE = 8
PAD = 4
SLOT = (0, 1, 3, 2)
LOW = -1e30
COEF = DH**-0.5 * math.log2(math.e)


def pieces_of(refs):
    for far in (0, 1):
        for t in range(4):
            for s in range(4):
                yield refs[4 * far + t], s * (CH + 16), s, t, far


def chunk_at(meta, s, yb, far):
    x, core = meta[0], meta[2]
    xb = (x - SLOT[s] + 4) % 4
    par = 1 - core if far else core
    return pl.multiple_of((2 * (4 * xb + yb) + par) * CH, CH)


def load_keys(refs, meta, k_s, v_s, kt_s, vt_s):
    for ref, first, s, t, far in pieces_of(refs):
        at = chunk_at(meta, s, (meta[1] - SLOT[t] + 4) % 4, far)
        kc = ref[first : first + CH, :DH]
        vc = ref[first : first + CH, DH:]
        k_s[pl.ds(at, CH), :] = kc
        if v_s is not None:
            v_s[pl.ds(at, CH), :] = vc
        if kt_s is not None:
            kt_s[:, pl.ds(at, CH)] = kc.T
        if vt_s is not None:
            vt_s[:, pl.ds(at, CH)] = vc.T
    tail = NB * CH
    k_s[tail:, :] = jnp.zeros((PAD * CH, DH), BF)
    if v_s is not None:
        v_s[tail:, :] = jnp.zeros((PAD * CH, DH), BF)
    if kt_s is not None:
        kt_s[:, tail:] = jnp.zeros((DH, PAD * CH), BF)
    if vt_s is not None:
        vt_s[:, tail:] = jnp.zeros((DH, PAD * CH), BF)


def doc_starts(refs):
    docs = jnp.concatenate(
        [ref[first + CH : first + CH + 16, :] for ref, first, _, _, _ in pieces_of(refs)], axis=0
    ).astype(F32)
    return [jnp.sum(jnp.where(docs < d, 1.0, 0.0)).astype(jnp.int32) for d in (1, 2, 3)]


def start_of(pos, starts):
    begin = jnp.zeros_like(pos)
    for c in starts:
        begin = jnp.where(pos >= c, c, begin)
    return begin


def group_facts(meta, gi, starts):
    x, y, core = meta[0], meta[1], meta[2]
    slot = gi // NG
    r = gi % NG
    back = jnp.where(slot == 2, 3, jnp.where(slot == 3, 2, slot))
    xs = (x - back + 4) % 4
    yb = jnp.where(r == 0, y, 3 - y)
    row0 = (8 * xs + 2 * yb + core) * ROWS + r * RG
    lane = lax.broadcasted_iota(jnp.int32, (1, L), 1)
    rpos = row0 + lane % RG
    ds = start_of(rpos, starts)
    ds_min = start_of(row0, starts)
    ds_max = start_of(row0 + RG - 1, starts)
    lo = (ds_min - CH * x + (ROWS - CH)) // ROWS
    end = (row0 + RG - 1 - CH * x + ROWS) // ROWS
    return slot, r, xs, row0, rpos, ds, ds_max, lo, jnp.maximum(0, end - lo)


def group_rows(ref, slot, r, which):
    at = pl.multiple_of(r * ROWS + which * HALF, HALF)
    both = ref[slot, pl.ds(at, HALF), :]
    return both[:, :DH], both[:, DH:]


def keep_of(m0, x, rpos, ds, step, causal=True, inside=True):
    base = m0 * ROWS + x * CH
    i = lax.broadcasted_iota(jnp.int32, (step * CH, 1), 0)
    kpos = base + i + (ROWS - CH) * (i // CH)
    if causal and inside:
        return (kpos <= rpos) & (kpos >= ds)
    return kpos <= rpos if causal else kpos >= ds


def by_mask(m0, x, row0, ds_max, step, work):
    first = m0 * ROWS + x * CH
    causal = first + (step - 1) * ROWS + CH - 1 > row0
    inside = first < ds_max
    for d in (False, True):
        if step < TILE:
            pl.when(inside == d)(functools.partial(work, True, d))
        else:
            for c in (False, True):
                pl.when((causal == c) & (inside == d))(functools.partial(work, c, d))


def over_tiles(lo, chunks, work):
    rest = chunks % TILE
    tiles = chunks // TILE + jnp.where(rest == 7, 1, 0)
    four = (rest >= 3) & (rest <= 6)
    two = (rest == 1) | (rest == 2) | (rest == 5) | (rest == 6)

    def whole(i, carry):
        work(lo + i * TILE, TILE)
        return carry

    lax.fori_loop(0, tiles, whole, 0)
    tail = lo + tiles * TILE
    pl.when(four)(lambda: work(tail, 4))
    pl.when(two)(lambda: work(tail + jnp.where(four, 4, 0), 2))


def mm(a, b):
    return jnp.dot(a, b, preferred_element_type=F32)


def forward_kernel(
    meta, n0, n1, n2, n3, f0, f1, f2, f3, qg_s,
    ot_ref, st_ref, k_s, vt_s, acc_s, m_s, l_s,
):
    x = meta[0]
    refs = (n0, n1, n2, n3, f0, f1, f2, f3)
    load_keys(refs, meta, k_s, None, None, vt_s)
    starts = doc_starts(refs)

    def group(gi, carry):
        slot, r, xs, row0, rpos, ds, ds_max, lo, chunks = group_facts(meta, gi, starts)
        q0, q1 = group_rows(qg_s, slot, r, 0)
        qt = jnp.concatenate([q0.T, q1.T], axis=1)
        acc_s[...] = jnp.zeros_like(acc_s)
        m_s[...] = jnp.zeros_like(m_s)
        l_s[...] = jnp.zeros_like(l_s)

        def tile(m0, step):
            here = pl.ds(pl.multiple_of(m0 * CH, CH), step * CH)

            def work(causal, inside):
                p = jnp.exp2(mm(k_s[here, :], qt) * COEF)
                if causal or inside:
                    p = jnp.where(keep_of(m0, x, rpos, ds, step, causal, inside), p, 0.0)
                l_s[...] += jnp.sum(p, axis=0, keepdims=True)
                acc_s[...] += mm(vt_s[:, here], p.astype(BF))

            by_mask(m0, x, row0, ds_max, step, work)

        over_tiles(lo, chunks, tile)

        def careful_tile(i, carry):
            step = 4
            m0 = lo + i * step
            here = pl.ds(pl.multiple_of(m0 * CH, CH), step * CH)
            keep = keep_of(m0, x, rpos, ds, step)
            s = jnp.where(keep, mm(k_s[here, :], qt), LOW)
            m_old = m_s[...]
            m_new = jnp.maximum(m_old, jnp.max(s, axis=0, keepdims=True) * COEF)
            alpha = jnp.exp2(m_old - m_new)
            p = jnp.where(keep, jnp.exp2(s * COEF - m_new), 0.0)
            l_s[...] = l_s[...] * alpha + jnp.sum(p, axis=0, keepdims=True)
            m_s[...] = m_new
            acc_s[...] = acc_s[...] * alpha + mm(vt_s[:, here], p.astype(BF))
            return carry

        block = (rpos - CH * x) >> 9
        last = jnp.minimum(rpos, block * ROWS + CH * x + CH - 1)
        some = (block >= 0) & (last >= ds)
        l = l_s[...]
        good = (jnp.min(jnp.where(some, l, 1.0)) >= 2.0**-60) & (jnp.max(l) <= 2.0**60)

        @pl.when(jnp.logical_not(good))
        def careful():
            acc_s[...] = jnp.zeros_like(acc_s)
            m_s[...] = jnp.full_like(m_s, LOW)
            l_s[...] = jnp.zeros_like(l_s)
            lax.fori_loop(0, (chunks + 3) // 4, careful_tile, 0)

        g0, g1 = group_rows(qg_s, slot, r, 1)
        gt = jnp.concatenate([g0.T, g1.T], axis=1).astype(F32)
        acc = acc_s[...]
        l = l_s[...]
        lanes = pl.ds(pl.multiple_of(r * L, L), L)
        ot_ref[slot, :, lanes] = (acc / jnp.where(l > 0, l, 1.0)).astype(BF)
        st_ref[xs, 0:1, lanes] = m_s[...]
        st_ref[xs, 1:2, lanes] = l
        st_ref[xs, 2:3, lanes] = jnp.sum(acc * gt, axis=0, keepdims=True)
        return carry

    lax.fori_loop(0, 4 * NG, group, 0)


def merged(sts):
    top = functools.reduce(jnp.maximum, [st[0:1] for st in sts])
    scale = [jnp.exp2(st[0:1] - top) for st in sts]
    total = sum(st[1:2] * f for st, f in zip(sts, scale))
    delta = sum(st[2:3] * f for st, f in zip(sts, scale)) / total
    return top + jnp.log2(total), delta, sts[0][1:2] * scale[0] / total


def backward_kernel(
    meta, n0, n1, n2, n3, f0, f1, f2, f3, qg_s,
    ot_ref, s0, s1, s2, s3, e0, e1, e2, e3a, e3b, mine_ref, theirs_ref,
    k_s, v_s, kt_s, dk_s, dv_s, acc_s, back_s,
):
    x = meta[0]
    refs = (n0, n1, n2, n3, f0, f1, f2, f3)
    load_keys(refs, meta, k_s, v_s, kt_s, None)
    starts = doc_starts(refs)
    dk_s[...] = jnp.zeros_like(dk_s)
    dv_s[...] = jnp.zeros_like(dv_s)

    def group(gi, carry):
        slot, r, xs, row0, rpos, ds, ds_max, lo, chunks = group_facts(meta, gi, starts)
        q0, q1 = group_rows(qg_s, slot, r, 0)
        g0, g1 = group_rows(qg_s, slot, r, 1)
        qt = jnp.concatenate([q0.T, q1.T], axis=1)
        gt = jnp.concatenate([g0.T, g1.T], axis=1)
        qm = jnp.concatenate([q0, q1], axis=0)
        gm = jnp.concatenate([g0, g1], axis=0)
        lanes = pl.ds(pl.multiple_of(r * L, L), L)
        lse, delta, share = merged([st[xs, :, lanes] for st in (s0, s1, s2, s3)])
        acc_s[...] = jnp.zeros_like(acc_s)

        def tile(m0, step):
            here = pl.ds(pl.multiple_of(m0 * CH, CH), step * CH)

            def work(causal, inside):
                s = mm(k_s[here, :], qt)
                p = jnp.exp2(s * COEF - lse)
                if causal or inside:
                    p = jnp.where(keep_of(m0, x, rpos, ds, step, causal, inside), p, 0.0)
                dp = mm(v_s[here, :], gt)
                dsc = (p * (dp - delta)).astype(BF)
                dv_s[here, :] += mm(p.astype(BF), gm)
                dk_s[here, :] += mm(dsc, qm)
                acc_s[...] += mm(kt_s[:, here], dsc)

            by_mask(m0, x, row0, ds_max, step, work)

        over_tiles(lo, chunks, tile)
        acc = acc_s[...]
        out = ot_ref[slot, :, lanes].astype(F32) * share
        for h in range(HH):
            cols = slice(h * DH, (h + 1) * DH)
            part = slice(h * RG, (h + 1) * RG)
            for k, value in enumerate((acc, out)):
                at = pl.multiple_of(r * ROWS + k * HALF, HALF)
                back_s[slot, pl.ds(at, HALF), cols] = value[:, part].T.astype(BF)
        return carry

    lax.fori_loop(0, 4 * NG, group, 0)
    for slot, ref in enumerate((e0, e1, e2)):
        ref[...] = back_s[slot]
    e3a[...] = back_s[3, :ROWS]
    e3b[...] = back_s[3, ROWS:]
    for t in range(4):
        yb = (meta[1] - SLOT[t] + 4) % 4
        for s in range(4):
            for far, ref in ((0, mine_ref), (1, theirs_ref)):
                at = pl.ds(chunk_at(meta, s, yb, far), CH)
                ref[t, s, :, :DH] = dk_s[at, :].astype(BF)
                ref[t, s, :, DH:] = dv_s[at, :].astype(BF)


def pack_kernel(meta, keys_hbm, values_hbm, docs_hbm, o0, o1, o2, o3, keys_ref, values_ref, docs_ref, sems):
    outs = (o0, o1, o2, o3)
    fetch(((keys_hbm, keys_ref), (values_hbm, values_ref), (docs_hbm, docs_ref)), sems)
    rest = jnp.full((16 - ROWS // DH, DH), 3.0, F32)
    docs = jnp.concatenate([docs_ref[...].astype(F32), rest], axis=0)
    docs = jnp.concatenate([docs, jnp.full((16, DH), 3.0, F32)], axis=1).astype(BF)
    for s, ref in enumerate(outs):
        at = pl.ds(pl.multiple_of((meta[0] + SLOT[s]) % 4 * CH, CH), CH)
        ref[:CH, :DH] = keys_ref[at, :]
        ref[:CH, DH:] = values_ref[at, :]
        ref[CH:, :] = docs


def fetch(pairs, sems):
    copies = [pltpu.make_async_copy(a, b, sems.at[i]) for i, (a, b) in enumerate(pairs)]
    for c in copies:
        c.start()
    for c in copies:
        c.wait()


def half_kernel(q_ref, g_ref, out_ref, sems):
    low, high = pl.ds(0, HALF), pl.ds(HALF, HALF)
    fetch(((q_ref.at[high], out_ref.at[low]), (g_ref.at[high], out_ref.at[high])), sems)


def pair_kernel(q_ref, g_ref, half_ref, after1, after2, after3, out_ref):
    out_ref[:HALF] = q_ref[:HALF]
    out_ref[HALF:ROWS] = g_ref[:HALF]
    out_ref[ROWS:] = half_ref[...]


def stack_kernel(p0, p1, p2, p3a, p3b, out_ref):
    for s, ref in enumerate((p0, p1, p2)):
        out_ref[s] = ref[...]
    out_ref[3, :ROWS] = p3a[...]
    out_ref[3, ROWS:] = p3b[...]


def join_kernel(mine_ref, theirs_ref, *outs):
    for t, ref in enumerate(outs):
        ref[...] = (mine_ref[t].astype(F32) + theirs_ref[t].astype(F32)).astype(BF)


def split_kernel(meta, p0, p1, p2, p3, *outs):
    for k, ref in enumerate(outs):
        s = (meta[3] + SLOT[k]) % 4
        ref[...] = sum(p[s].astype(F32) for p in (p0, p1, p2, p3)).astype(BF)


def sum_kernel(p0, p1, p2, p3, out_ref):
    out_ref[...] = sum(p[...].astype(F32) for p in (p0, p1, p2, p3)).astype(BF)


def place_kernel(meta, p0, p1, p2, p3, dk_ref, dv_ref):
    for k, ref in enumerate((p0, p1, p2, p3)):
        s = (meta[3] - k + 4) % 4
        step = jnp.where(s == 2, 3, jnp.where(s == 3, 2, s))
        at = pl.ds(pl.multiple_of((meta[0] + step) % 4 * CH, CH), CH)
        dk_ref[at, :] = ref[:, :DH].astype(F32) * DH**-0.5
        dv_ref[at, :] = ref[:, DH:].astype(F32)


def relay_kernel(e1, e2, ra, rb, after, o1, o2):
    o1[:ROWS] = (e1[:ROWS].astype(F32) + ra[...].astype(F32)).astype(BF)
    o1[ROWS:] = e1[ROWS:]
    o2[:ROWS] = e2[:ROWS]
    o2[ROWS:] = (e2[ROWS:].astype(F32) + rb[...].astype(F32)).astype(BF)


def far_kernel(p0, p1, p2, out_ref):
    out_ref[...] = sum(p[ROWS:].astype(F32) for p in (p0, p1, p2)).astype(BF)


def finish_kernel(p0, p1, p2, half_ref, out_ref, dq_ref):
    for k, ref, scale in ((0, dq_ref, DH**-0.5), (1, out_ref, 1.0)):
        at = slice(k * HALF, (k + 1) * HALF)
        total = sum(p[at].astype(F32) for p in (p0, p1, p2))
        ref[:HALF] = (total * scale).astype(ref.dtype)
        ref[HALF:] = (half_ref[at].astype(F32) * scale).astype(ref.dtype)


SMEM = pl.BlockSpec(memory_space=pltpu.SMEM)
ANY = pl.BlockSpec(memory_space=pl.ANY)
VMEM = pl.BlockSpec(memory_space=pltpu.VMEM)
WIDE = pltpu.CompilerParams(vmem_limit_bytes=60 * 1024 * 1024)
PARAMS = pltpu.CompilerParams(vmem_limit_bytes=32 * 1024 * 1024)
SDS = jax.ShapeDtypeStruct


def cost(us, size):
    return pl.CostEstimate(flops=us * 10**9, bytes_accessed=size, transcendentals=0)


def call(kernel, name, us, n_in, outs, scratch=(), smem=True, space=None):
    return pl.pallas_call(
        kernel,
        in_specs=[SMEM] * smem + [space or VMEM] * n_in,
        out_specs=[VMEM] * len(outs),
        out_shape=outs,
        scratch_shapes=list(scratch),
        compiler_params=WIDE if space else PARAMS,
        cost_estimate=cost(us, 1 << 20),
        name=name,
    )


KEYS_S = pltpu.VMEM(((NB + PAD) * CH, DH), BF)
TURN_S = pltpu.VMEM((DH, (NB + PAD) * CH), BF)
GRAD_S = pltpu.VMEM(((NB + PAD) * CH, DH), F32)
ACC_S = pltpu.VMEM((DH, L), F32)
LINE_S = pltpu.VMEM((1, L), F32)


def run_forward(meta, keys, rows):
    return call(
        forward_kernel,
        "forward",
        12,
        9,
        [SDS((4, DH, HH * ROWS), BF), SDS((4, 3, HH * ROWS), F32)],
        [KEYS_S, TURN_S, ACC_S, LINE_S, LINE_S],
    )(meta, *keys, rows)


def run_backward(meta, keys, rows, ot, stats):
    *back, mine, theirs = call(
        backward_kernel,
        "backward",
        25,
        14,
        [SDS((2 * ROWS, HH * DH), BF)] * 3
        + [SDS((ROWS, HH * DH), BF)] * 2
        + [SDS((4, 4, CH, 2 * DH), BF)] * 2,
        [KEYS_S, KEYS_S, TURN_S, GRAD_S, GRAD_S, ACC_S]
        + [pltpu.VMEM((4, 2 * ROWS, HH * DH), BF)],
    )(meta, *keys, rows, ot, *stats)
    return back, mine, theirs


def shift(value, axis, by):
    return lax.ppermute(value, axis, [(i, (i + by) % 4) for i in range(4)])


def swap(value):
    return lax.ppermute(value, "core", [(0, 1), (1, 0)])


def gathered(value, axis):
    return [value] + [shift(value, axis, by) for by in SLOT[1:]]


def mirrored(value):
    return lax.ppermute(value, "y", [(i, 3 - i) for i in range(4)])


def ring(value, axis):
    half = value.shape[0] // 2
    one, two = shift(value, axis, 1), shift(value, axis, 3)
    return [value, one, two, shift(one[:half], axis, 1), shift(two[half:], axis, 3)]


def sent_back(slots, axis):
    return [slots[0]] + [shift(slots[s], axis, 4 - SLOT[s]) for s in (1, 2, 3)]


def local(queries, keys, values, doc_ids, out_grad):
    meta = jnp.stack([lax.axis_index(a) for a in ("x", "y", "core", "z")]).astype(jnp.int32)
    packed = SDS((CH + 16, 2 * DH), BF)
    lent = [
        pltpu.VMEM((ROWS, DH), BF),
        pltpu.VMEM((ROWS, DH), BF),
        pltpu.VMEM((ROWS // DH, DH), jnp.int32),
        pltpu.SemaphoreType.DMA((3,)),
    ]
    chunks = call(pack_kernel, "pack", 1, 3, [packed] * 4, lent, space=ANY)(
        meta, keys, values, doc_ids.reshape(ROWS // DH, DH)
    )
    came = [shift(chunks[s], "x", SLOT[s]) for s in (1, 2, 3)]
    column = jnp.concatenate([chunks[0]] + came)
    near = gathered(column, "y")
    keys_all = near + [swap(n) for n in near]
    half = SDS((ROWS, HH * DH), BF)
    sems = [pltpu.SemaphoreType.DMA((2,))]
    second = call(half_kernel, "half", 1, 2, [half], sems, smem=False, space=ANY)(
        queries, out_grad
    )[0]
    both = call(pair_kernel, "pair", 1, 6, [SDS((2 * ROWS, HH * DH), BF)], smem=False)
    stack = call(stack_kernel, "stack", 1, 5, [SDS((4, 2 * ROWS, HH * DH), BF)], smem=False)
    rows = stack(*ring(both(queries, out_grad, mirrored(second), *came)[0], "x"))[0]
    ot, st = run_forward(meta, keys_all, rows)
    stats = gathered(st, "x")
    (e0, e1, e2, e3a, e3b), mine, theirs = run_backward(meta, keys_all, rows, ot, stats)
    column = SDS((4, CH, 2 * DH), BF)
    chunk = SDS((CH, 2 * DH), BF)
    terms = call(join_kernel, "join", 1, 2, [column] * 4, smem=False)(mine, swap(theirs))
    parts = call(split_kernel, "split", 8, 4, [chunk] * 4)(meta, *sent_back(terms, "y"))
    parts = [parts[0]] + [shift(parts[k], "z", SLOT[k]) for k in (1, 2, 3)]
    total = call(sum_kernel, "sum", 8, 4, [chunk], smem=False)(*parts)[0]
    every = [
        lax.ppermute(
            total,
            ("x", "z"),
            [
                (4 * a + z, (a - SLOT[z]) % 4 * 4 + (z + k) % 4)
                for a in range(4)
                for z in range(4)
            ],
        )
        for k in range(4)
    ]
    k_grad, v_grad = call(place_kernel, "place", 1, 4, [SDS((ROWS, DH), F32)] * 2)(meta, *every)
    relay = call(relay_kernel, "relay", 1, 5, [SDS((2 * ROWS, HH * DH), BF)] * 2, smem=False)
    e1, e2 = relay(e1, e2, shift(e3a, "x", 3), shift(e3b, "x", 1), terms[0])
    finish = call(
        finish_kernel,
        "finish",
        1,
        4,
        [SDS((ROWS, HH * DH), BF), SDS((ROWS, HH * DH), F32)],
        smem=False,
    )
    p1, p2 = shift(e1, "x", 3), shift(e2, "x", 1)
    second = call(far_kernel, "far", 1, 3, [half], smem=False)(e0, p1, p2)[0]
    attn_out, q_grad = finish(e0, p1, p2, mirrored(second))
    return attn_out, q_grad, k_grad, v_grad


def solution(mesh):
    fine = Mesh(mesh.devices.reshape(4, 4, 2, 4), ("x", "y", "core", "z"))
    ctx = ("x", "y", "core")
    return jax.shard_map(
        local,
        mesh=fine,
        in_specs=(P(ctx, "z"), P(ctx, None), P(ctx, None), P(ctx), P(ctx, "z")),
        out_specs=(P(ctx, "z"), P(ctx, "z"), P(ctx, None), P(ctx, None)),
        check_vma=False,
    )
```

```python
import functools
import math

import jax
import jax.numpy as jnp
from jax import lax
from jax.experimental import pallas as pl
from jax.experimental.pallas import tpu as pltpu
from jax.sharding import Mesh, PartitionSpec as P

BF = jnp.bfloat16
F32 = jnp.float32
DH = 128
ROWS = 512
CH = 128
NB = 32
HH = 2
RG = 512
NG = ROWS // RG
HALF = ROWS // 2
L = HH * RG
TILE = 8
PAD = 4
SLOT = (0, 1, 3, 2)
LOW = -1e30
COEF = DH**-0.5 * math.log2(math.e)


def pieces_of(refs):
    for far in (0, 1):
        for t in range(4):
            for s in range(4):
                yield refs[4 * far + t], s * (CH + 16), s, t, far


def chunk_at(meta, s, yb, far):
    x, core = meta[0], meta[2]
    xb = (x - SLOT[s] + 4) % 4
    par = 1 - core if far else core
    return pl.multiple_of((2 * (4 * xb + yb) + par) * CH, CH)


def load_keys(refs, meta, k_s, v_s, kt_s, vt_s):
    for ref, first, s, t, far in pieces_of(refs):
        at = chunk_at(meta, s, (meta[1] - SLOT[t] + 4) % 4, far)
        kc = ref[first : first + CH, :DH]
        vc = ref[first : first + CH, DH:]
        k_s[pl.ds(at, CH), :] = kc
        if v_s is not None:
            v_s[pl.ds(at, CH), :] = vc
        if kt_s is not None:
            kt_s[:, pl.ds(at, CH)] = kc.T
        if vt_s is not None:
            vt_s[:, pl.ds(at, CH)] = vc.T
    tail = NB * CH
    k_s[tail:, :] = jnp.zeros((PAD * CH, DH), BF)
    if v_s is not None:
        v_s[tail:, :] = jnp.zeros((PAD * CH, DH), BF)
    if kt_s is not None:
        kt_s[:, tail:] = jnp.zeros((DH, PAD * CH), BF)
    if vt_s is not None:
        vt_s[:, tail:] = jnp.zeros((DH, PAD * CH), BF)


def doc_starts(refs):
    docs = jnp.concatenate(
        [ref[first + CH : first + CH + 16, :] for ref, first, _, _, _ in pieces_of(refs)], axis=0
    ).astype(F32)
    return [jnp.sum(jnp.where(docs < d, 1.0, 0.0)).astype(jnp.int32) for d in (1, 2, 3)]


def start_of(pos, starts):
    begin = jnp.zeros_like(pos)
    for c in starts:
        begin = jnp.where(pos >= c, c, begin)
    return begin


def group_facts(meta, gi, starts):
    x, y, core = meta[0], meta[1], meta[2]
    slot = gi // NG
    r = gi % NG
    back = jnp.where(slot == 2, 3, jnp.where(slot == 3, 2, slot))
    xs = (x - back + 4) % 4
    row0 = (8 * xs + 2 * y + core) * ROWS + r * RG
    lane = lax.broadcasted_iota(jnp.int32, (1, L), 1)
    rpos = row0 + lane % RG
    ds = start_of(rpos, starts)
    ds_min = start_of(row0, starts)
    ds_max = start_of(row0 + RG - 1, starts)
    lo = (ds_min - CH * x + (ROWS - CH)) // ROWS
    end = (row0 + RG - 1 - CH * x + ROWS) // ROWS
    return slot, r, xs, row0, rpos, ds, ds_max, lo, jnp.maximum(0, end - lo)


def group_rows(ref, slot, which):
    at = which * HALF
    both = jnp.concatenate(
        [ref[slot, at : at + HALF, :], ref[slot, ROWS + at : ROWS + at + HALF, :]], axis=0
    )
    return both[:, :DH], both[:, DH:]


def keep_of(m0, x, rpos, ds, step, causal=True, inside=True):
    base = m0 * ROWS + x * CH
    i = lax.broadcasted_iota(jnp.int32, (step * CH, 1), 0)
    kpos = base + i + (ROWS - CH) * (i // CH)
    if causal and inside:
        return (kpos <= rpos) & (kpos >= ds)
    return kpos <= rpos if causal else kpos >= ds


def by_mask(m0, x, row0, ds_max, step, work):
    first = m0 * ROWS + x * CH
    causal = first + (step - 1) * ROWS + CH - 1 > row0
    inside = first < ds_max
    for d in (False, True):
        if step < TILE:
            pl.when(inside == d)(functools.partial(work, True, d))
        else:
            for c in (False, True):
                pl.when((causal == c) & (inside == d))(functools.partial(work, c, d))


def over_tiles(lo, chunks, work):
    rest = chunks % TILE
    tiles = chunks // TILE + jnp.where(rest == 7, 1, 0)
    four = (rest >= 3) & (rest <= 6)
    two = (rest == 1) | (rest == 2) | (rest == 5) | (rest == 6)

    def whole(i, carry):
        work(lo + i * TILE, TILE)
        return carry

    lax.fori_loop(0, tiles, whole, 0)
    tail = lo + tiles * TILE
    pl.when(four)(lambda: work(tail, 4))
    pl.when(two)(lambda: work(tail + jnp.where(four, 4, 0), 2))


def mm(a, b):
    return jnp.dot(a, b, preferred_element_type=F32)


def forward_kernel(
    meta, n0, n1, n2, n3, f0, f1, f2, f3, qg_s,
    ot_ref, st_ref, k_s, vt_s, acc_s, m_s, l_s,
):
    x = meta[0]
    refs = (n0, n1, n2, n3, f0, f1, f2, f3)
    load_keys(refs, meta, k_s, None, None, vt_s)
    starts = doc_starts(refs)

    def group(gi, carry):
        slot, r, xs, row0, rpos, ds, ds_max, lo, chunks = group_facts(meta, gi, starts)
        q0, q1 = group_rows(qg_s, slot, 0)
        qt = jnp.concatenate([q0.T, q1.T], axis=1)
        acc_s[...] = jnp.zeros_like(acc_s)
        m_s[...] = jnp.zeros_like(m_s)
        l_s[...] = jnp.zeros_like(l_s)

        def tile(m0, step):
            here = pl.ds(pl.multiple_of(m0 * CH, CH), step * CH)

            def work(causal, inside):
                p = jnp.exp2(mm(k_s[here, :], qt) * COEF)
                if causal or inside:
                    p = jnp.where(keep_of(m0, x, rpos, ds, step, causal, inside), p, 0.0)
                l_s[...] += jnp.sum(p, axis=0, keepdims=True)
                acc_s[...] += mm(vt_s[:, here], p.astype(BF))

            by_mask(m0, x, row0, ds_max, step, work)

        over_tiles(lo, chunks, tile)

        def careful_tile(i, carry):
            step = 4
            m0 = lo + i * step
            here = pl.ds(pl.multiple_of(m0 * CH, CH), step * CH)
            keep = keep_of(m0, x, rpos, ds, step)
            s = jnp.where(keep, mm(k_s[here, :], qt), LOW)
            m_old = m_s[...]
            m_new = jnp.maximum(m_old, jnp.max(s, axis=0, keepdims=True) * COEF)
            alpha = jnp.exp2(m_old - m_new)
            p = jnp.where(keep, jnp.exp2(s * COEF - m_new), 0.0)
            l_s[...] = l_s[...] * alpha + jnp.sum(p, axis=0, keepdims=True)
            m_s[...] = m_new
            acc_s[...] = acc_s[...] * alpha + mm(vt_s[:, here], p.astype(BF))
            return carry

        block = (rpos - CH * x) >> 9
        last = jnp.minimum(rpos, block * ROWS + CH * x + CH - 1)
        some = (block >= 0) & (last >= ds)
        l = l_s[...]
        good = (jnp.min(jnp.where(some, l, 1.0)) >= 2.0**-60) & (jnp.max(l) <= 2.0**60)

        @pl.when(jnp.logical_not(good))
        def careful():
            acc_s[...] = jnp.zeros_like(acc_s)
            m_s[...] = jnp.full_like(m_s, LOW)
            l_s[...] = jnp.zeros_like(l_s)
            lax.fori_loop(0, (chunks + 3) // 4, careful_tile, 0)

        g0, g1 = group_rows(qg_s, slot, 1)
        gt = jnp.concatenate([g0.T, g1.T], axis=1).astype(F32)
        acc = acc_s[...]
        l = l_s[...]
        lanes = pl.ds(pl.multiple_of(r * L, L), L)
        ot_ref[slot, :, lanes] = (acc / jnp.where(l > 0, l, 1.0)).astype(BF)
        st_ref[xs, 0:1, lanes] = m_s[...]
        st_ref[xs, 1:2, lanes] = l
        st_ref[xs, 2:3, lanes] = jnp.sum(acc * gt, axis=0, keepdims=True)
        return carry

    lax.fori_loop(0, 4 * NG, group, 0)


def merged(sts):
    top = functools.reduce(jnp.maximum, [st[0:1] for st in sts])
    scale = [jnp.exp2(st[0:1] - top) for st in sts]
    total = sum(st[1:2] * f for st, f in zip(sts, scale))
    delta = sum(st[2:3] * f for st, f in zip(sts, scale)) / total
    return top + jnp.log2(total), delta, sts[0][1:2] * scale[0] / total


def backward_kernel(
    meta, n0, n1, n2, n3, f0, f1, f2, f3, qg_s,
    ot_ref, s0, s1, s2, s3, e0, e1, e2, e3a, e3b, mine_ref, theirs_ref,
    k_s, v_s, kt_s, dk_s, dv_s, acc_s, back_s,
):
    x = meta[0]
    refs = (n0, n1, n2, n3, f0, f1, f2, f3)
    load_keys(refs, meta, k_s, v_s, kt_s, None)
    starts = doc_starts(refs)
    dk_s[...] = jnp.zeros_like(dk_s)
    dv_s[...] = jnp.zeros_like(dv_s)

    def group(gi, carry):
        slot, r, xs, row0, rpos, ds, ds_max, lo, chunks = group_facts(meta, gi, starts)
        q0, q1 = group_rows(qg_s, slot, 0)
        g0, g1 = group_rows(qg_s, slot, 1)
        qt = jnp.concatenate([q0.T, q1.T], axis=1)
        gt = jnp.concatenate([g0.T, g1.T], axis=1)
        qm = jnp.concatenate([q0, q1], axis=0)
        gm = jnp.concatenate([g0, g1], axis=0)
        lanes = pl.ds(pl.multiple_of(r * L, L), L)
        lse, delta, share = merged([st[xs, :, lanes] for st in (s0, s1, s2, s3)])
        acc_s[...] = jnp.zeros_like(acc_s)

        def tile(m0, step):
            here = pl.ds(pl.multiple_of(m0 * CH, CH), step * CH)

            def work(causal, inside):
                s = mm(k_s[here, :], qt)
                p = jnp.exp2(s * COEF - lse)
                if causal or inside:
                    p = jnp.where(keep_of(m0, x, rpos, ds, step, causal, inside), p, 0.0)
                dp = mm(v_s[here, :], gt)
                dsc = (p * (dp - delta)).astype(BF)
                dv_s[here, :] += mm(p.astype(BF), gm)
                dk_s[here, :] += mm(dsc, qm)
                acc_s[...] += mm(kt_s[:, here], dsc)

            by_mask(m0, x, row0, ds_max, step, work)

        over_tiles(lo, chunks, tile)
        acc = acc_s[...]
        out = ot_ref[slot, :, lanes].astype(F32) * share
        for h in range(HH):
            cols = slice(h * DH, (h + 1) * DH)
            for n in range(2):
                part = slice(h * RG + n * HALF, h * RG + (n + 1) * HALF)
                back_s[slot, (2 * n) * HALF : (2 * n + 1) * HALF, cols] = acc[:, part].T.astype(BF)
                back_s[slot, (2 * n + 1) * HALF : (2 * n + 2) * HALF, cols] = out[:, part].T.astype(BF)
        return carry

    lax.fori_loop(0, 4 * NG, group, 0)
    for slot, ref in enumerate((e0, e1, e2)):
        ref[...] = back_s[slot]
    e3a[...] = back_s[3, :ROWS]
    e3b[...] = back_s[3, ROWS:]
    for t in range(4):
        yb = (meta[1] - SLOT[t] + 4) % 4
        for s in range(4):
            for far, ref in ((0, mine_ref), (1, theirs_ref)):
                at = pl.ds(chunk_at(meta, s, yb, far), CH)
                ref[t, s, :, :DH] = dk_s[at, :].astype(BF)
                ref[t, s, :, DH:] = dv_s[at, :].astype(BF)


def pack_kernel(meta, keys_ref, values_ref, docs_ref, *outs):
    rest = jnp.full((16 - ROWS // DH, DH), 3.0, F32)
    docs = jnp.concatenate([docs_ref[...].astype(F32), rest], axis=0)
    docs = jnp.concatenate([docs, jnp.full((16, DH), 3.0, F32)], axis=1).astype(BF)
    for s, ref in enumerate(outs):
        at = pl.ds(pl.multiple_of((meta[0] + SLOT[s]) % 4 * CH, CH), CH)
        ref[:CH, :DH] = keys_ref[at, :]
        ref[:CH, DH:] = values_ref[at, :]
        ref[CH:, :] = docs


def column_kernel(c0, c1, c2, c3, out_ref):
    for s, ref in enumerate((c0, c1, c2, c3)):
        out_ref[s * (CH + 16) : (s + 1) * (CH + 16)] = ref[...]


def pair_kernel(q_ref, g_ref, after, out_ref):
    for n in range(2):
        here = slice(n * HALF, (n + 1) * HALF)
        out_ref[2 * n * HALF : (2 * n + 1) * HALF] = q_ref[here]
        out_ref[(2 * n + 1) * HALF : (2 * n + 2) * HALF] = g_ref[here]


def stack_kernel(p0, p1, p2, p3a, p3b, out_ref):
    for s, ref in enumerate((p0, p1, p2)):
        out_ref[s] = ref[...]
    out_ref[3, :ROWS] = p3a[...]
    out_ref[3, ROWS:] = p3b[...]


def join_kernel(mine_ref, theirs_ref, *outs):
    for t, ref in enumerate(outs):
        ref[...] = (mine_ref[t].astype(F32) + theirs_ref[t].astype(F32)).astype(BF)


def split_kernel(meta, p0, p1, p2, p3, *outs):
    for k, ref in enumerate(outs):
        s = (meta[3] + SLOT[k]) % 4
        ref[...] = sum(p[s].astype(F32) for p in (p0, p1, p2, p3)).astype(BF)


def sum_kernel(p0, p1, p2, p3, out_ref):
    out_ref[...] = sum(p[...].astype(F32) for p in (p0, p1, p2, p3)).astype(BF)


def place_kernel(meta, p0, p1, p2, p3, dk_ref, dv_ref):
    for k, ref in enumerate((p0, p1, p2, p3)):
        s = (meta[3] - k + 4) % 4
        step = jnp.where(s == 2, 3, jnp.where(s == 3, 2, s))
        at = pl.ds(pl.multiple_of((meta[0] + step) % 4 * CH, CH), CH)
        dk_ref[at, :] = ref[:, :DH].astype(F32) * DH**-0.5
        dv_ref[at, :] = ref[:, DH:].astype(F32)


def relay_kernel(e1, e2, ra, rb, after, o1, o2):
    o1[:ROWS] = (e1[:ROWS].astype(F32) + ra[...].astype(F32)).astype(BF)
    o1[ROWS:] = e1[ROWS:]
    o2[:ROWS] = e2[:ROWS]
    o2[ROWS:] = (e2[ROWS:].astype(F32) + rb[...].astype(F32)).astype(BF)


def finish_kernel(p0, p1, p2, out_ref, dq_ref):
    for n in range(2):
        here = slice(n * HALF, (n + 1) * HALF)
        for k, ref in ((0, dq_ref), (1, out_ref)):
            at = slice((2 * n + k) * HALF, (2 * n + k + 1) * HALF)
            total = sum(p[at].astype(F32) for p in (p0, p1, p2))
            ref[here] = (total if k else total * DH**-0.5).astype(ref.dtype)


SMEM = pl.BlockSpec(memory_space=pltpu.SMEM)
VMEM = pl.BlockSpec(memory_space=pltpu.VMEM)
PARAMS = pltpu.CompilerParams(vmem_limit_bytes=32 * 1024 * 1024)
SDS = jax.ShapeDtypeStruct


def cost(us, size):
    return pl.CostEstimate(flops=us * 10**9, bytes_accessed=size, transcendentals=0)


def call(kernel, name, us, n_in, outs, scratch=(), smem=True):
    return pl.pallas_call(
        kernel,
        in_specs=[SMEM] * smem + [VMEM] * n_in,
        out_specs=[VMEM] * len(outs),
        out_shape=outs,
        scratch_shapes=list(scratch),
        compiler_params=PARAMS,
        cost_estimate=cost(us, 1 << 20),
        name=name,
    )


KEYS_S = pltpu.VMEM(((NB + PAD) * CH, DH), BF)
TURN_S = pltpu.VMEM((DH, (NB + PAD) * CH), BF)
GRAD_S = pltpu.VMEM(((NB + PAD) * CH, DH), F32)
ACC_S = pltpu.VMEM((DH, L), F32)
LINE_S = pltpu.VMEM((1, L), F32)


def run_forward(meta, keys, rows):
    return call(
        forward_kernel,
        "forward",
        12,
        9,
        [SDS((4, DH, HH * ROWS), BF), SDS((4, 3, HH * ROWS), F32)],
        [KEYS_S, TURN_S, ACC_S, LINE_S, LINE_S],
    )(meta, *keys, rows)


def run_backward(meta, keys, rows, ot, stats):
    *back, mine, theirs = call(
        backward_kernel,
        "backward",
        25,
        14,
        [SDS((2 * ROWS, HH * DH), BF)] * 3
        + [SDS((ROWS, HH * DH), BF)] * 2
        + [SDS((4, 4, CH, 2 * DH), BF)] * 2,
        [KEYS_S, KEYS_S, TURN_S, GRAD_S, GRAD_S, ACC_S]
        + [pltpu.VMEM((4, 2 * ROWS, HH * DH), BF)],
    )(meta, *keys, rows, ot, *stats)
    return back, mine, theirs


def shift(value, axis, by):
    return lax.ppermute(value, axis, [(i, (i + by) % 4) for i in range(4)])


def swap(value):
    return lax.ppermute(value, "core", [(0, 1), (1, 0)])


def gathered(value, axis):
    return [value] + [shift(value, axis, by) for by in SLOT[1:]]


def ring(value, axis):
    half = value.shape[0] // 2
    one, two = shift(value, axis, 1), shift(value, axis, 3)
    return [value, one, two, shift(one[:half], axis, 1), shift(two[half:], axis, 3)]


def sent_back(slots, axis):
    return [slots[0]] + [shift(slots[s], axis, 4 - SLOT[s]) for s in (1, 2, 3)]


def local(queries, keys, values, doc_ids, out_grad):
    meta = jnp.stack([lax.axis_index(a) for a in ("x", "y", "core", "z")]).astype(jnp.int32)
    packed = SDS((CH + 16, 2 * DH), BF)
    chunks = call(pack_kernel, "pack", 1, 3, [packed] * 4)(
        meta, keys, values, doc_ids.reshape(ROWS // DH, DH)
    )
    came = [shift(chunks[s], "x", SLOT[s]) for s in (1, 2, 3)]
    column = SDS((4 * (CH + 16), 2 * DH), BF)
    column = call(column_kernel, "column", 12, 4, [column], smem=False)(chunks[0], *came)[0]
    near = gathered(column, "y")
    keys_all = near + [swap(n) for n in near]
    both = call(pair_kernel, "pair", 1, 3, [SDS((2 * ROWS, HH * DH), BF)], smem=False)
    stack = call(stack_kernel, "stack", 1, 5, [SDS((4, 2 * ROWS, HH * DH), BF)], smem=False)
    rows = stack(*ring(both(queries, out_grad, chunks[0])[0], "x"))[0]
    ot, st = run_forward(meta, keys_all, rows)
    stats = gathered(st, "x")
    (e0, e1, e2, e3a, e3b), mine, theirs = run_backward(meta, keys_all, rows, ot, stats)
    column = SDS((4, CH, 2 * DH), BF)
    chunk = SDS((CH, 2 * DH), BF)
    terms = call(join_kernel, "join", 1, 2, [column] * 4, smem=False)(mine, swap(theirs))
    parts = call(split_kernel, "split", 8, 4, [chunk] * 4)(meta, *sent_back(terms, "y"))
    parts = [parts[0]] + [shift(parts[k], "z", SLOT[k]) for k in (1, 2, 3)]
    relay = call(relay_kernel, "relay", 1, 5, [SDS((2 * ROWS, HH * DH), BF)] * 2, smem=False)
    e1, e2 = relay(e1, e2, shift(e3a, "x", 3), shift(e3b, "x", 1), terms[0])
    finish = call(
        finish_kernel,
        "finish",
        1,
        3,
        [SDS((ROWS, HH * DH), BF), SDS((ROWS, HH * DH), F32)],
        smem=False,
    )
    attn_out, q_grad = finish(e0, shift(e1, "x", 3), shift(e2, "x", 1))
    attn_out, q_grad, *parts = lax.optimization_barrier((attn_out, q_grad, *parts))
    total = call(sum_kernel, "sum", 8, 4, [chunk], smem=False)(*parts)[0]
    every = [
        lax.ppermute(
            total,
            ("x", "z"),
            [
                (4 * a + z, (a - SLOT[z]) % 4 * 4 + (z + k) % 4)
                for a in range(4)
                for z in range(4)
            ],
        )
        for k in range(4)
    ]
    k_grad, v_grad = call(place_kernel, "place", 1, 4, [SDS((ROWS, DH), F32)] * 2)(meta, *every)
    return attn_out, q_grad, k_grad, v_grad


def solution(mesh):
    fine = Mesh(mesh.devices.reshape(4, 4, 2, 4), ("x", "y", "core", "z"))
    ctx = ("x", "y", "core")
    return jax.shard_map(
        local,
        mesh=fine,
        in_specs=(P(ctx, "z"), P(ctx, None), P(ctx, None), P(ctx), P(ctx, "z")),
        out_specs=(P(ctx, "z"), P(ctx, "z"), P(ctx, None), P(ctx, None)),
        check_vma=False,
    )
```

```python
import functools
import math

import jax
import jax.numpy as jnp
from jax import lax
from jax.experimental import pallas as pl
from jax.experimental.pallas import tpu as pltpu
from jax.sharding import Mesh, PartitionSpec as P

BF = jnp.bfloat16
F32 = jnp.float32
DH = 128
ROWS = 512
CH = 128
NB = 32
HH = 2
RG = 512
NG = ROWS // RG
HALF = ROWS // 2
L = HH * RG
TILE = 4
PAD = 4
SLOT = (0, 1, 3, 2)
LOW = -1e30
COEF = DH**-0.5 * math.log2(math.e)


def pieces_of(refs):
    for far in (0, 1):
        for t in range(4):
            for s in range(4):
                yield refs[4 * far + t], s * (CH + 16), s, t, far


def chunk_at(meta, s, yb, far):
    x, core = meta[0], meta[2]
    xb = (x - SLOT[s] + 4) % 4
    par = 1 - core if far else core
    return pl.multiple_of((2 * (4 * xb + yb) + par) * CH, CH)


def load_keys(refs, meta, k_s, v_s, kt_s, vt_s):
    for ref, first, s, t, far in pieces_of(refs):
        at = chunk_at(meta, s, (meta[1] - SLOT[t] + 4) % 4, far)
        kc = ref[first : first + CH, :DH]
        vc = ref[first : first + CH, DH:]
        k_s[pl.ds(at, CH), :] = kc
        if v_s is not None:
            v_s[pl.ds(at, CH), :] = vc
        if kt_s is not None:
            kt_s[:, pl.ds(at, CH)] = kc.T
        if vt_s is not None:
            vt_s[:, pl.ds(at, CH)] = vc.T
    tail = NB * CH
    k_s[tail:, :] = jnp.zeros((PAD * CH, DH), BF)
    if v_s is not None:
        v_s[tail:, :] = jnp.zeros((PAD * CH, DH), BF)
    if kt_s is not None:
        kt_s[:, tail:] = jnp.zeros((DH, PAD * CH), BF)
    if vt_s is not None:
        vt_s[:, tail:] = jnp.zeros((DH, PAD * CH), BF)


def doc_starts(refs):
    docs = jnp.concatenate(
        [ref[first + CH : first + CH + 16, :] for ref, first, _, _, _ in pieces_of(refs)], axis=0
    ).astype(F32)
    return [jnp.sum(jnp.where(docs < d, 1.0, 0.0)).astype(jnp.int32) for d in (1, 2, 3)]


def start_of(pos, starts):
    begin = jnp.zeros_like(pos)
    for c in starts:
        begin = jnp.where(pos >= c, c, begin)
    return begin


def group_facts(meta, gi, starts):
    x, y, core = meta[0], meta[1], meta[2]
    slot = gi // NG
    r = gi % NG
    back = jnp.where(slot == 2, 3, jnp.where(slot == 3, 2, slot))
    xs = (x - back + 4) % 4
    row0 = (8 * xs + 2 * y + core) * ROWS + r * RG
    lane = lax.broadcasted_iota(jnp.int32, (1, L), 1)
    rpos = row0 + lane % RG
    ds = start_of(rpos, starts)
    ds_min = start_of(row0, starts)
    ds_max = start_of(row0 + RG - 1, starts)
    lo = (ds_min - CH * x + (ROWS - CH)) // ROWS
    end = (row0 + RG - 1 - CH * x + ROWS) // ROWS
    return slot, r, xs, row0, rpos, ds, ds_max, lo, jnp.maximum(0, end - lo)


def group_rows(ref, slot, which):
    at = which * HALF
    both = jnp.concatenate(
        [ref[slot, at : at + HALF, :], ref[slot, ROWS + at : ROWS + at + HALF, :]], axis=0
    )
    return both[:, :DH], both[:, DH:]


def keep_of(m0, x, rpos, ds, step, causal=True, inside=True):
    base = m0 * ROWS + x * CH
    i = lax.broadcasted_iota(jnp.int32, (step * CH, 1), 0)
    kpos = base + i + (ROWS - CH) * (i // CH)
    if causal and inside:
        return (kpos <= rpos) & (kpos >= ds)
    return kpos <= rpos if causal else kpos >= ds


def by_mask(m0, x, row0, ds_max, step, work):
    first = m0 * ROWS + x * CH
    causal = first + (step - 1) * ROWS + CH - 1 > row0
    inside = first < ds_max
    for c in (False, True):
        for d in (False, True):
            pl.when((causal == c) & (inside == d))(functools.partial(work, c, d))


def over_tiles(lo, chunks, work):
    tiles = (chunks + 1) // TILE
    tail = chunks - tiles * TILE

    def whole(i, carry):
        work(lo + i * TILE, TILE)
        return carry

    lax.fori_loop(0, tiles, whole, 0)

    @pl.when(tail > 0)
    def rest():
        work(lo + tiles * TILE, TILE // 2)


def mm(a, b):
    return jnp.dot(a, b, preferred_element_type=F32)


def forward_kernel(
    meta, n0, n1, n2, n3, f0, f1, f2, f3, qg_s,
    ot_ref, st_ref, k_s, vt_s, acc_s, m_s, l_s,
):
    x = meta[0]
    refs = (n0, n1, n2, n3, f0, f1, f2, f3)
    load_keys(refs, meta, k_s, None, None, vt_s)
    starts = doc_starts(refs)

    def group(gi, carry):
        slot, r, xs, row0, rpos, ds, ds_max, lo, chunks = group_facts(meta, gi, starts)
        q0, q1 = group_rows(qg_s, slot, 0)
        qt = jnp.concatenate([q0.T, q1.T], axis=1)
        acc_s[...] = jnp.zeros_like(acc_s)
        m_s[...] = jnp.zeros_like(m_s)
        l_s[...] = jnp.zeros_like(l_s)

        def tile(m0, step):
            here = pl.ds(pl.multiple_of(m0 * CH, CH), step * CH)

            def work(causal, inside):
                p = jnp.exp2(mm(k_s[here, :], qt) * COEF)
                if causal or inside:
                    p = jnp.where(keep_of(m0, x, rpos, ds, step, causal, inside), p, 0.0)
                l_s[...] += jnp.sum(p, axis=0, keepdims=True)
                acc_s[...] += mm(vt_s[:, here], p.astype(BF))

            by_mask(m0, x, row0, ds_max, step, work)

        over_tiles(lo, chunks, tile)

        def careful_tile(i, carry):
            step = TILE // 2
            m0 = lo + i * step
            here = pl.ds(pl.multiple_of(m0 * CH, CH), step * CH)
            keep = keep_of(m0, x, rpos, ds, step)
            s = jnp.where(keep, mm(k_s[here, :], qt), LOW)
            m_old = m_s[...]
            m_new = jnp.maximum(m_old, jnp.max(s, axis=0, keepdims=True) * COEF)
            alpha = jnp.exp2(m_old - m_new)
            p = jnp.where(keep, jnp.exp2(s * COEF - m_new), 0.0)
            l_s[...] = l_s[...] * alpha + jnp.sum(p, axis=0, keepdims=True)
            m_s[...] = m_new
            acc_s[...] = acc_s[...] * alpha + mm(vt_s[:, here], p.astype(BF))
            return carry

        block = (rpos - CH * x) >> 9
        last = jnp.minimum(rpos, block * ROWS + CH * x + CH - 1)
        some = (block >= 0) & (last >= ds)
        l = l_s[...]
        good = (jnp.min(jnp.where(some, l, 1.0)) >= 2.0**-60) & (jnp.max(l) <= 2.0**60)

        @pl.when(jnp.logical_not(good))
        def careful():
            acc_s[...] = jnp.zeros_like(acc_s)
            m_s[...] = jnp.full_like(m_s, LOW)
            l_s[...] = jnp.zeros_like(l_s)
            lax.fori_loop(0, (chunks + TILE // 2 - 1) // (TILE // 2), careful_tile, 0)

        g0, g1 = group_rows(qg_s, slot, 1)
        gt = jnp.concatenate([g0.T, g1.T], axis=1).astype(F32)
        acc = acc_s[...]
        l = l_s[...]
        lanes = pl.ds(pl.multiple_of(r * L, L), L)
        ot_ref[slot, :, lanes] = (acc / jnp.where(l > 0, l, 1.0)).astype(BF)
        st_ref[xs, 0:1, lanes] = m_s[...]
        st_ref[xs, 1:2, lanes] = l
        st_ref[xs, 2:3, lanes] = jnp.sum(acc * gt, axis=0, keepdims=True)
        return carry

    lax.fori_loop(0, 4 * NG, group, 0)


def merged(sts):
    top = functools.reduce(jnp.maximum, [st[0:1] for st in sts])
    scale = [jnp.exp2(st[0:1] - top) for st in sts]
    total = sum(st[1:2] * f for st, f in zip(sts, scale))
    delta = sum(st[2:3] * f for st, f in zip(sts, scale)) / total
    return top + jnp.log2(total), delta, sts[0][1:2] * scale[0] / total


def backward_kernel(
    meta, n0, n1, n2, n3, f0, f1, f2, f3, qg_s,
    ot_ref, s0, s1, s2, s3, e0, e1, e2, e3a, e3b, mine_ref, theirs_ref,
    k_s, v_s, kt_s, dk_s, dv_s, acc_s, back_s,
):
    x = meta[0]
    refs = (n0, n1, n2, n3, f0, f1, f2, f3)
    load_keys(refs, meta, k_s, v_s, kt_s, None)
    starts = doc_starts(refs)
    dk_s[...] = jnp.zeros_like(dk_s)
    dv_s[...] = jnp.zeros_like(dv_s)

    def group(gi, carry):
        slot, r, xs, row0, rpos, ds, ds_max, lo, chunks = group_facts(meta, gi, starts)
        q0, q1 = group_rows(qg_s, slot, 0)
        g0, g1 = group_rows(qg_s, slot, 1)
        qt = jnp.concatenate([q0.T, q1.T], axis=1)
        gt = jnp.concatenate([g0.T, g1.T], axis=1)
        qm = jnp.concatenate([q0, q1], axis=0)
        gm = jnp.concatenate([g0, g1], axis=0)
        lanes = pl.ds(pl.multiple_of(r * L, L), L)
        lse, delta, share = merged([st[xs, :, lanes] for st in (s0, s1, s2, s3)])
        acc_s[...] = jnp.zeros_like(acc_s)

        def tile(m0, step):
            here = pl.ds(pl.multiple_of(m0 * CH, CH), step * CH)

            def work(causal, inside):
                s = mm(k_s[here, :], qt)
                p = jnp.exp2(s * COEF - lse)
                if causal or inside:
                    p = jnp.where(keep_of(m0, x, rpos, ds, step, causal, inside), p, 0.0)
                dp = mm(v_s[here, :], gt)
                dsc = (p * (dp - delta)).astype(BF)
                dv_s[here, :] += mm(p.astype(BF), gm)
                dk_s[here, :] += mm(dsc, qm)
                acc_s[...] += mm(kt_s[:, here], dsc)

            by_mask(m0, x, row0, ds_max, step, work)

        over_tiles(lo, chunks, tile)
        acc = acc_s[...]
        out = ot_ref[slot, :, lanes].astype(F32) * share
        for h in range(HH):
            cols = slice(h * DH, (h + 1) * DH)
            for n in range(2):
                part = slice(h * RG + n * HALF, h * RG + (n + 1) * HALF)
                back_s[slot, (2 * n) * HALF : (2 * n + 1) * HALF, cols] = acc[:, part].T.astype(BF)
                back_s[slot, (2 * n + 1) * HALF : (2 * n + 2) * HALF, cols] = out[:, part].T.astype(BF)
        return carry

    lax.fori_loop(0, 4 * NG, group, 0)
    for slot, ref in enumerate((e0, e1, e2)):
        ref[...] = back_s[slot]
    e3a[...] = back_s[3, :ROWS]
    e3b[...] = back_s[3, ROWS:]
    for t in range(4):
        yb = (meta[1] - SLOT[t] + 4) % 4
        for s in range(4):
            for far, ref in ((0, mine_ref), (1, theirs_ref)):
                at = pl.ds(chunk_at(meta, s, yb, far), CH)
                ref[t, s, :, :DH] = dk_s[at, :].astype(BF)
                ref[t, s, :, DH:] = dv_s[at, :].astype(BF)


def pack_kernel(meta, keys_ref, values_ref, docs_ref, *outs):
    rest = jnp.full((16 - ROWS // DH, DH), 3.0, F32)
    docs = jnp.concatenate([docs_ref[...].astype(F32), rest], axis=0)
    docs = jnp.concatenate([docs, jnp.full((16, DH), 3.0, F32)], axis=1).astype(BF)
    for s, ref in enumerate(outs):
        at = pl.ds(pl.multiple_of((meta[0] + SLOT[s]) % 4 * CH, CH), CH)
        ref[:CH, :DH] = keys_ref[at, :]
        ref[:CH, DH:] = values_ref[at, :]
        ref[CH:, :] = docs


def column_kernel(c0, c1, c2, c3, out_ref):
    for s, ref in enumerate((c0, c1, c2, c3)):
        out_ref[s * (CH + 16) : (s + 1) * (CH + 16)] = ref[...]


def pair_kernel(q_ref, g_ref, after, out_ref):
    for n in range(2):
        here = slice(n * HALF, (n + 1) * HALF)
        out_ref[2 * n * HALF : (2 * n + 1) * HALF] = q_ref[here]
        out_ref[(2 * n + 1) * HALF : (2 * n + 2) * HALF] = g_ref[here]


def stack_kernel(p0, p1, p2, p3a, p3b, out_ref):
    for s, ref in enumerate((p0, p1, p2)):
        out_ref[s] = ref[...]
    out_ref[3, :ROWS] = p3a[...]
    out_ref[3, ROWS:] = p3b[...]


def join_kernel(mine_ref, theirs_ref, *outs):
    for t, ref in enumerate(outs):
        ref[...] = (mine_ref[t].astype(F32) + theirs_ref[t].astype(F32)).astype(BF)


def split_kernel(meta, p0, p1, p2, p3, *outs):
    for k, ref in enumerate(outs):
        s = (meta[3] + SLOT[k]) % 4
        ref[...] = sum(p[s].astype(F32) for p in (p0, p1, p2, p3)).astype(BF)


def sum_kernel(p0, p1, p2, p3, out_ref):
    out_ref[...] = sum(p[...].astype(F32) for p in (p0, p1, p2, p3)).astype(BF)


def place_kernel(meta, p0, p1, p2, p3, dk_ref, dv_ref):
    for k, ref in enumerate((p0, p1, p2, p3)):
        s = (meta[3] - k + 4) % 4
        step = jnp.where(s == 2, 3, jnp.where(s == 3, 2, s))
        at = pl.ds(pl.multiple_of((meta[0] + step) % 4 * CH, CH), CH)
        dk_ref[at, :] = ref[:, :DH].astype(F32) * DH**-0.5
        dv_ref[at, :] = ref[:, DH:].astype(F32)


def relay_kernel(e1, e2, ra, rb, after, o1, o2):
    o1[:ROWS] = (e1[:ROWS].astype(F32) + ra[...].astype(F32)).astype(BF)
    o1[ROWS:] = e1[ROWS:]
    o2[:ROWS] = e2[:ROWS]
    o2[ROWS:] = (e2[ROWS:].astype(F32) + rb[...].astype(F32)).astype(BF)


def finish_kernel(p0, p1, p2, out_ref, dq_ref):
    for n in range(2):
        here = slice(n * HALF, (n + 1) * HALF)
        for k, ref in ((0, dq_ref), (1, out_ref)):
            at = slice((2 * n + k) * HALF, (2 * n + k + 1) * HALF)
            total = sum(p[at].astype(F32) for p in (p0, p1, p2))
            ref[here] = (total if k else total * DH**-0.5).astype(ref.dtype)


SMEM = pl.BlockSpec(memory_space=pltpu.SMEM)
VMEM = pl.BlockSpec(memory_space=pltpu.VMEM)
PARAMS = pltpu.CompilerParams(vmem_limit_bytes=32 * 1024 * 1024)
SDS = jax.ShapeDtypeStruct


def cost(us, size):
    return pl.CostEstimate(flops=us * 10**9, bytes_accessed=size, transcendentals=0)


def call(kernel, name, us, n_in, outs, scratch=(), smem=True):
    return pl.pallas_call(
        kernel,
        in_specs=[SMEM] * smem + [VMEM] * n_in,
        out_specs=[VMEM] * len(outs),
        out_shape=outs,
        scratch_shapes=list(scratch),
        compiler_params=PARAMS,
        cost_estimate=cost(us, 1 << 20),
        name=name,
    )


KEYS_S = pltpu.VMEM(((NB + PAD) * CH, DH), BF)
TURN_S = pltpu.VMEM((DH, (NB + PAD) * CH), BF)
GRAD_S = pltpu.VMEM(((NB + PAD) * CH, DH), F32)
ACC_S = pltpu.VMEM((DH, L), F32)
LINE_S = pltpu.VMEM((1, L), F32)


def run_forward(meta, keys, rows):
    return call(
        forward_kernel,
        "forward",
        12,
        9,
        [SDS((4, DH, HH * ROWS), BF), SDS((4, 3, HH * ROWS), F32)],
        [KEYS_S, TURN_S, ACC_S, LINE_S, LINE_S],
    )(meta, *keys, rows)


def run_backward(meta, keys, rows, ot, stats):
    *back, mine, theirs = call(
        backward_kernel,
        "backward",
        25,
        14,
        [SDS((2 * ROWS, HH * DH), BF)] * 3
        + [SDS((ROWS, HH * DH), BF)] * 2
        + [SDS((4, 4, CH, 2 * DH), BF)] * 2,
        [KEYS_S, KEYS_S, TURN_S, GRAD_S, GRAD_S, ACC_S]
        + [pltpu.VMEM((4, 2 * ROWS, HH * DH), BF)],
    )(meta, *keys, rows, ot, *stats)
    return back, mine, theirs


def shift(value, axis, by):
    return lax.ppermute(value, axis, [(i, (i + by) % 4) for i in range(4)])


def swap(value):
    return lax.ppermute(value, "core", [(0, 1), (1, 0)])


def gathered(value, axis):
    return [value] + [shift(value, axis, by) for by in SLOT[1:]]


def ring(value, axis):
    half = value.shape[0] // 2
    one, two = shift(value, axis, 1), shift(value, axis, 3)
    return [value, one, two, shift(one[:half], axis, 1), shift(two[half:], axis, 3)]


def sent_back(slots, axis):
    return [slots[0]] + [shift(slots[s], axis, 4 - SLOT[s]) for s in (1, 2, 3)]


def local(queries, keys, values, doc_ids, out_grad):
    meta = jnp.stack([lax.axis_index(a) for a in ("x", "y", "core", "z")]).astype(jnp.int32)
    packed = SDS((CH + 16, 2 * DH), BF)
    chunks = call(pack_kernel, "pack", 1, 3, [packed] * 4)(
        meta, keys, values, doc_ids.reshape(ROWS // DH, DH)
    )
    came = [shift(chunks[s], "x", SLOT[s]) for s in (1, 2, 3)]
    column = SDS((4 * (CH + 16), 2 * DH), BF)
    column = call(column_kernel, "column", 12, 4, [column], smem=False)(chunks[0], *came)[0]
    near = gathered(column, "y")
    keys_all = near + [swap(n) for n in near]
    both = call(pair_kernel, "pair", 1, 3, [SDS((2 * ROWS, HH * DH), BF)], smem=False)
    stack = call(stack_kernel, "stack", 1, 5, [SDS((4, 2 * ROWS, HH * DH), BF)], smem=False)
    rows = stack(*ring(both(queries, out_grad, chunks[0])[0], "x"))[0]
    ot, st = run_forward(meta, keys_all, rows)
    stats = gathered(st, "x")
    (e0, e1, e2, e3a, e3b), mine, theirs = run_backward(meta, keys_all, rows, ot, stats)
    column = SDS((4, CH, 2 * DH), BF)
    chunk = SDS((CH, 2 * DH), BF)
    terms = call(join_kernel, "join", 1, 2, [column] * 4, smem=False)(mine, swap(theirs))
    parts = call(split_kernel, "split", 8, 4, [chunk] * 4)(meta, *sent_back(terms, "y"))
    parts = [parts[0]] + [shift(parts[k], "z", SLOT[k]) for k in (1, 2, 3)]
    relay = call(relay_kernel, "relay", 1, 5, [SDS((2 * ROWS, HH * DH), BF)] * 2, smem=False)
    e1, e2 = relay(e1, e2, shift(e3a, "x", 3), shift(e3b, "x", 1), terms[0])
    finish = call(
        finish_kernel,
        "finish",
        1,
        3,
        [SDS((ROWS, HH * DH), BF), SDS((ROWS, HH * DH), F32)],
        smem=False,
    )
    attn_out, q_grad = finish(e0, shift(e1, "x", 3), shift(e2, "x", 1))
    attn_out, q_grad, *parts = lax.optimization_barrier((attn_out, q_grad, *parts))
    total = call(sum_kernel, "sum", 8, 4, [chunk], smem=False)(*parts)[0]
    every = [
        lax.ppermute(
            total,
            ("x", "z"),
            [
                (4 * a + z, (a - SLOT[z]) % 4 * 4 + (z + k) % 4)
                for a in range(4)
                for z in range(4)
            ],
        )
        for k in range(4)
    ]
    k_grad, v_grad = call(place_kernel, "place", 1, 4, [SDS((ROWS, DH), F32)] * 2)(meta, *every)
    return attn_out, q_grad, k_grad, v_grad


def solution(mesh):
    fine = Mesh(mesh.devices.reshape(4, 4, 2, 4), ("x", "y", "core", "z"))
    ctx = ("x", "y", "core")
    return jax.shard_map(
        local,
        mesh=fine,
        in_specs=(P(ctx, "z"), P(ctx, None), P(ctx, None), P(ctx), P(ctx, "z")),
        out_specs=(P(ctx, "z"), P(ctx, "z"), P(ctx, None), P(ctx, None)),
        check_vma=False,
    )
```
